512 devices in a mesh: shot: 8 (over z_lo, core), gx: 16 (over x, y), gy: 4 (over z_hi).
Axes of the slice: x: 4, y: 4, z: 16 (z_hi: 4, z_lo: 4; z = z_hi * 4 + z_lo), core: 2. Of those that a mesh axis runs over, the one named last changes fastest.
Arguments:
- velocity: float32 [16, 256, 512], P('shot', 'gx', 'gy'), may hold values from 0.5 to 1
- buoyancy: float32 [16, 256, 512], P('shot', 'gx', 'gy'), may hold values from 0.5 to 1
- fwd_field: bfloat16 [8, 8, 16, 256, 512], P('shot', None, None, 'gx', 'gy'), may hold values from -6 to 6
- adjoint_now: float32 [8, 16, 256, 512], P('shot', None, 'gx', 'gy'), may hold values from -6 to 6
- adjoint_prev: float32 [8, 16, 256, 512], P('shot', None, 'gx', 'gy'), may hold values from -6 to 6
- recv_cell: int32 [8, 256], P('shot'), may hold values from 0 to 2097151
- traces: float32 [8, 8, 256], P('shot'), may hold values from -6 to 6
Outputs:
- grad_vel: float32 [16, 256, 512], P('shot', 'gx', 'gy')
- grad_buoy: float32 [16, 256, 512], P('shot', 'gx', 'gy')
- adjoint_out: float32 [8, 16, 256, 512], P('shot', None, 'gx', 'gy')
- adjoint_out_prev: float32 [8, 16, 256, 512], P('shot', None, 'gx', 'gy')
The draws below stay inside these ranges and needn't reach their ends.
Inputs may be any that keep to these rules, and one draw needn't show every extreme that they name: `recv_cell`: z*256*512 + x*512 + y of a cell inside the grid.
All inputs are finite; a program needn't handle non-finite values.
Results may differ from the reference program's by a relative error of at most 0.0003.
Values sent between devices are 32-bit elements; how exact they have to be, the bound alone decides.
No kernel may reach another device: no remote copies, remote signals or barrier semaphores. Data moves between devices by JAX's collectives and lax.ppermute only.
A program may use at most 64 MiB of HBM per device.

```python
import jax
import jax.numpy as jnp
from jax import lax

NZ = 16
STEPS = 8
RECV = 256
NX = 256
NY = 512
SHOTS = 8


def with_ends(drawn, stream_key, smallest, largest):
    longest = drawn.shape.index(max(drawn.shape))
    spots = []
    for shift in (0, 1):
        where = [jax.random.randint(jax.random.fold_in(stream_key, axis), (), 0, length) for axis, length in enumerate(drawn.shape)]
        where[longest] = (where[longest] + shift) % drawn.shape[longest]
        spots.append(tuple(where))
    return drawn.at[spots[0]].set(smallest).at[spots[1]].set(largest)


def block_scale(stream_key, dims, shards, smallest, top_value):
    loudness, own = 1.0, jax.random.fold_in(stream_key, 6)
    for dim, blocks in shards:
        draws = jnp.exp(jax.random.uniform(jax.random.fold_in(own, dim), (blocks,), jnp.float32, smallest / len(shards), top_value / len(shards)))
        loudness = loudness * jnp.repeat(draws, dims[dim] // blocks).reshape([-1 if axis == dim else 1 for axis in range(len(dims))])
    return loudness


def normal_values(stream_key, dims, scale, reach, pieces=(), kind=jnp.bfloat16):
    entries = scale * jax.random.normal(stream_key, dims, jnp.float32)
    if pieces:
        entries = entries * block_scale(stream_key, dims, pieces, -0.22, 0.18)
    return jnp.clip(entries, -reach, reach).astype(kind)


def setup_inputs(seed: int = 0) -> dict:
    seeds = jax.random.split(jax.random.key(seed), 8)
    velocity = jnp.clip(0.5 + 0.5 * jax.random.uniform(seeds[0], (NZ, NX, NY), jnp.float32) ** block_scale(seeds[0], (NZ, NX, NY), ((0, 8), (1, 16), (2, 4)), -0.2, 0.2), 0.5, 1.0)
    buoyancy = jnp.clip(0.5 + 0.5 * jax.random.uniform(seeds[1], (NZ, NX, NY), jnp.float32) ** block_scale(seeds[1], (NZ, NX, NY), ((0, 8), (1, 16), (2, 4)), -0.2, 0.2), 0.5, 1.0)
    fwd_field = normal_values(seeds[2], (SHOTS, STEPS, NZ, NX, NY), 1.0, 6.0, ((0, 8), (3, 16), (4, 4)))
    adjoint_now = normal_values(seeds[3], (SHOTS, NZ, NX, NY), 1.0, 6.0, ((0, 8), (2, 16), (3, 4)), jnp.float32)
    adjoint_prev = normal_values(seeds[4], (SHOTS, NZ, NX, NY), 1.0, 6.0, ((0, 8), (2, 16), (3, 4)), jnp.float32)
    recv_cell = with_ends(jax.random.randint(seeds[5], (SHOTS, RECV), 0, NZ * NX * NY), jax.random.fold_in(seeds[5], 1), 0, (NZ * NX * NY) - 1).astype(jnp.int32)
    traces = normal_values(seeds[6], (SHOTS, STEPS, RECV), 1.0, 6.0, ((0, 8),), jnp.float32)
    return dict(velocity=velocity, buoyancy=buoyancy, fwd_field=fwd_field, adjoint_now=adjoint_now, adjoint_prev=adjoint_prev, recv_cell=recv_cell, traces=traces)


second_coef = (-205.0 / 72.0, 8.0 / 5.0, -1.0 / 5.0, 8.0 / 315.0, -1.0 / 560.0)
first_coef = (4.0 / 5.0, -1.0 / 5.0, 4.0 / 105.0, -1.0 / 280.0)
courant = 0.15


def derivs(padded):
    nz = padded.shape[-3]
    length_x = padded.shape[-2] - 8
    length_y = padded.shape[-1] - 8
    zpadded = jnp.pad(padded, [(0, 0)] * (padded.ndim - 3) + [(4, 4), (0, 0), (0, 0)])

    def cut(dz, dx, dy):
        return zpadded[..., 4 + dz:4 + dz + nz, 4 + dx:4 + dx + length_x, 4 + dy:4 + dy + length_y]

    lap = (3.0 * second_coef[0]) * cut(0, 0, 0)
    grad_z = jnp.zeros_like(lap)
    grad_x = jnp.zeros_like(lap)
    grad_y = jnp.zeros_like(lap)
    for k in range(1, 5):
        lap = lap + second_coef[k] * (cut(k, 0, 0) + cut(-k, 0, 0) + cut(0, k, 0) + cut(0, -k, 0) + cut(0, 0, k) + cut(0, 0, -k))
        grad_z = grad_z + first_coef[k - 1] * (cut(k, 0, 0) - cut(-k, 0, 0))
        grad_x = grad_x + first_coef[k - 1] * (cut(0, k, 0) - cut(0, -k, 0))
        grad_y = grad_y + first_coef[k - 1] * (cut(0, 0, k) - cut(0, 0, -k))
    return lap, grad_z, grad_x, grad_y


def pad_sides(field):
    return jnp.pad(field, [(0, 0)] * (field.ndim - 2) + [(4, 4), (4, 4)])


def reference(velocity, buoyancy, fwd_field, adjoint_now, adjoint_prev, recv_cell, traces):
    unused, bgrad_z, bgrad_x, bgrad_y = derivs(pad_sides(buoyancy))
    speed = courant * velocity * velocity
    depth_idx = recv_cell // (NX * NY)
    rest = recv_cell % (NX * NY)
    x_idx = rest // NY
    y_idx = rest % NY

    def one_shot(inputs):
        now, prev, forward, depth_s, x_s, y_s, trace_s = inputs
        image_v = jnp.zeros((NZ, NX, NY), jnp.float32)
        image_b = jnp.zeros((NZ, NX, NY), jnp.float32)
        for step in range(STEPS):
            field = now.at[depth_s, x_s, y_s].add(trace_s[step])
            lap, grad_z, grad_x, grad_y = derivs(pad_sides(field))
            operated = buoyancy * lap + bgrad_z * grad_z + bgrad_x * grad_x + bgrad_y * grad_y
            snapshot = forward[step].astype(jnp.float32)
            image_v = image_v + snapshot * operated
            image_b = image_b + snapshot * lap
            now = 2.0 * field - prev + speed * operated
            prev = field
        return now, prev, image_v, image_b

    now_all, prev_all, images_v, images_b = lax.map(one_shot, (adjoint_now, adjoint_prev, fwd_field, depth_idx, x_idx, y_idx, traces))
    scale = 1.0 / (SHOTS * STEPS) ** 0.5
    grad_vel = 2.0 * courant * velocity * jnp.sum(images_v, axis=0) * scale
    grad_buoy = courant * velocity * velocity * jnp.sum(images_b, axis=0) * scale
    return grad_vel, grad_buoy, now_all, prev_all
```

```python
import functools

import jax
import jax.numpy as jnp
from jax import lax
from jax.experimental import pallas as pl
from jax.experimental.pallas import tpu as pltpu
from jax.sharding import PartitionSpec as P

NZ, BX, BY = 16, 16, 128
FULL_X, FULL_Y = 256, 512
STEPS, SHOTS, RECV = 8, 8, 256
ROUND = 4
HY = 32
EXT = 3 * BX
PAD = 8
ROWS = EXT + 2 * PAD
LAYERS = NZ + 8
FAR = BY - HY

second_coef = (-205.0 / 72.0, 8.0 / 5.0, -1.0 / 5.0, 8.0 / 315.0, -1.0 / 560.0)
first_coef = (4.0 / 5.0, -1.0 / 5.0, 4.0 / 105.0, -1.0 / 280.0)
courant = 0.15

VM = pl.BlockSpec(memory_space=pltpu.VMEM)
SM = pl.BlockSpec(memory_space=pltpu.SMEM)


def lane_of(rows):
    return lax.broadcasted_iota(jnp.int32, (rows, BY), 1)


def find_kernel(where_ref, recv_ref, place_ref, which_ref, count_ref):
    base_x = where_ref[0] - BX
    base_y = where_ref[1]

    def body(j, count):
        cell = recv_ref[j]
        z = lax.shift_right_logical(cell, 17)
        x = (lax.shift_right_logical(cell, 9) & (FULL_X - 1)) - base_x
        y = (cell & (FULL_Y - 1)) - base_y
        inside = (x >= 0) & (x < EXT) & (y >= -HY) & (y < BY + HY)
        place_ref[count] = z * 16384 + (x & 63) * 256 + (y & 255)
        which_ref[count] = j
        return count + inside.astype(jnp.int32)

    count_ref[0] = lax.fori_loop(0, RECV, body, jnp.int32(0))


def pack_kernel(where_ref, now_ref, prev_ref, model_ref, first_ref, second_ref):
    even = where_ref[2] == 0
    lane = lane_of(BX)
    out = 0
    for ref in (now_ref, prev_ref, model_ref):
        for q in range(ref.shape[0] // 4):
            right = left = jnp.zeros((BX, BY), jnp.float32)
            for j in range(4):
                plane = ref[4 * q + j]
                mine = (lane >= HY * j) & (lane < HY * (j + 1))
                right = jnp.where(mine, pltpu.roll(plane, (HY * j + HY) % BY, 1), right)
                left = jnp.where(mine, pltpu.roll(plane, HY * j, 1) if j else plane, left)
            first_ref[out] = jnp.where(even, right, left)
            second_ref[out] = jnp.where(even, left, right)
            out += 1


def rolled(main, side, lane, shift):
    a = pltpu.roll(main, -shift % BY, 1)
    b = pltpu.roll(side, -shift % BY, 1)
    keep = lane < BY - shift if shift > 0 else lane >= -shift
    return jnp.where(keep, a, b), jnp.where(keep, b, a)


def derivs(main, side, z, lo, n, sides=True):
    refs = (main, side)
    row = PAD + lo
    centre = [r[z + 4, pl.ds(row, n), :] for r in refs]
    lane = lane_of(n)
    use = (0, 1) if sides else (0,)
    lap = [3.0 * second_coef[0] * centre[i] for i in use]
    dz, dx, dy = [None, None], [None, None], [None, None]
    for k in range(1, 5):
        up = rolled(*centre, lane, k)
        down = rolled(*centre, lane, -k)
        for i in use:
            r = refs[i]
            zp = r[z + 4 + k, pl.ds(row, n), :]
            zm = r[z + 4 - k, pl.ds(row, n), :]
            xp = r[z + 4, pl.ds(row + k, n), :]
            xm = r[z + 4, pl.ds(row - k, n), :]
            lap[i] += second_coef[k] * (((zp + zm) + (xp + xm)) + (up[i] + down[i]))
            for total, p, m in ((dz, zp, zm), (dx, xp, xm), (dy, up[i], down[i])):
                term = first_coef[k - 1] * (p - m)
                total[i] = term if total[i] is None else total[i] + term
    return lap, dz, dx, dy


def run_steps(first_step, cur, old, coefs, fwd_ref, image, place_ref, which_ref, count_ref, trace_ref, last):
    speed, buoy, bz, bx, by = coefs
    plans = (
        ((0, 16), (16, 16), (32, 16)),
        ((8, 8), (16, 16), (32, 8)),
        ((8, 8), (16, 16), (32, 8)),
        ((16, 16),),
    )
    lane1 = lane_of(1)
    for j, plan in enumerate(plans):
        step = first_step + j

        def add(i, _, cur=cur, step=step):
            place = place_ref[i]
            value = trace_ref[step, which_ref[i]]
            z = lax.shift_right_logical(place, 14) + 4
            x = (lax.shift_right_logical(place, 8) & 63) + PAD
            y = place & 255
            for t in (0, 1):
                spot = (z, pl.ds(x, 1), slice(None))
                cur[t][spot] = cur[t][spot] + jnp.where(lane1 + BY * t == y, value, 0.0)
            return 0

        lax.fori_loop(0, count_ref[0], add, 0)
        sides = not (last and j == ROUND - 1)

        def layer(z, _, cur=cur, old=old, plan=plan, j=j, sides=sides):
            for lo, n in plan:
                lap, dz, dx, dy = derivs(cur[0], cur[1], z, lo, n, sides)
                rows = pl.ds(lo, n)
                for i in (0, 1) if sides else (0,):
                    operated = (
                        buoy[i][z + 4, pl.ds(lo + PAD, n), :] * lap[i]
                        + bz[i][z, rows, :] * dz[i]
                        + bx[i][z, rows, :] * dx[i]
                        + by[i][z, rows, :] * dy[i]
                    )
                    spot = (z + 4, pl.ds(lo + PAD, n), slice(None))
                    old[i][spot] = (2.0 * cur[i][spot] - old[i][spot]) + speed[i][z, rows, :] * operated
                    if i == 0 and lo == BX:
                        snapshot = fwd_ref[j, z].astype(jnp.float32)
                        image[0][z] += snapshot * operated
                        image[1][z] += snapshot * lap[0]
            return 0

        lax.fori_loop(0, NZ, layer, 0)
        cur, old = old, cur
    return cur, old


def clear(ref):
    def body(z, _):
        ref[z] = jnp.zeros(ref.shape[1:], jnp.float32)
        return 0

    lax.fori_loop(0, ref.shape[0], body, 0)


def unpack(first, second, even, lane, j):
    right = jnp.where(even, first, second)
    left = jnp.where(even, second, first)
    right = pltpu.roll(right, -HY * j % BY, 1) if j else right
    left = pltpu.roll(left, (FAR - HY * j) % BY, 1) if j < 3 else left
    return jnp.where(lane < HY, right, jnp.where(lane >= FAR, left, 0.0))


def first_kernel(
    where_ref, place_ref, which_ref, count_ref, trace_ref,
    centre_ref, low_ref, high_ref, other_ref, fwd_ref,
    send_ref, iv_ref, ib_ref,
    s0, s1, b0, b1, bz0, bz1, bx0, bx1, by0, by1,
    cm, cs, om, os_,
):
    even = where_ref[2] == 0
    core = where_ref[3]
    lane = lane_of(BX)
    for ref in (cm, cs, om, os_, b0, b1):
        clear(ref)
    for block, ref in enumerate((low_ref, centre_ref, high_ref)):
        rows = pl.ds(PAD + block * BX, BX)
        for f, (main, side) in enumerate(((cm, cs), (om, os_))):
            for q in range(4):
                a, b = ref[48 + 4 * f + q], ref[60 + 4 * f + q]
                for j in range(4):
                    z = 4 * q + j
                    main[4 + z, rows, :] = ref[NZ * f + z]
                    side[4 + z, rows, :] = unpack(a, b, even, lane, j)
        for half in (0, 1):
            turn = core if half == 0 else 1 - core
            spot = (1, 0, 2)[block]
            for q in range(4):
                if half == 0:
                    a, b = ref[56 + q], ref[68 + q]
                else:
                    a, b = other_ref[24 * spot + 16 + q], other_ref[24 * spot + 20 + q]
                for j in range(4):
                    plane = ref[32 + 4 * q + j] if half == 0 else other_ref[24 * spot + 4 * q + j]
                    edge = unpack(a, b, even, lane, j)
                    z = 4 * q + 2 * turn + j % 2
                    if j < 2:
                        s0[z, pl.ds(block * BX, BX), :] = courant * plane * plane
                        s1[z, pl.ds(block * BX, BX), :] = courant * edge * edge
                    else:
                        b0[4 + z, rows, :] = plane
                        b1[4 + z, rows, :] = edge

    def slopes(z, _):
        for lo, n in ((0, 16), (16, 16), (32, 16)):
            _, dz, dx, dy = derivs(b0, b1, z, lo, n)
            for pair, d in (((bz0, bz1), dz), ((bx0, bx1), dx), ((by0, by1), dy)):
                for i in (0, 1):
                    pair[i][z, pl.ds(lo, n), :] = d[i]
        return 0

    lax.fori_loop(0, NZ, slopes, 0)
    clear(iv_ref)
    clear(ib_ref)
    cur, old = run_steps(
        0, (cm, cs), (om, os_), ((s0, s1), (b0, b1), (bz0, bz1), (bx0, bx1), (by0, by1)),
        fwd_ref, (iv_ref, ib_ref), place_ref, which_ref, count_ref, trace_ref, False,
    )
    rows = pl.ds(PAD + BX, BX)
    for f, (main, side) in enumerate((cur, old)):
        for q in range(4):
            total = jnp.zeros((BX, BY), jnp.float32)
            for j in range(4):
                z = 4 * q + j
                send_ref[NZ * f + z] = main[4 + z, rows, :]
                mine = (lane >= HY * j) & (lane < HY * (j + 1))
                total = jnp.where(mine, pltpu.roll(side[4 + z, rows, :], (16 + HY * j) % BY, 1), total)
            send_ref[32 + 4 * f + q] = total


def second_kernel(
    place_ref, which_ref, count_ref, trace_ref,
    centre_ref, low_ref, high_ref, fwd_ref, iv_ref, ib_ref,
    s0, s1, b0, b1, bz0, bz1, bx0, bx1, by0, by1,
    now_ref, prev_ref, images_ref,
    cm, cs, om, os_, iv, ib,
):
    lane = lane_of(BX)
    for ref in (cm, cs, om, os_):
        clear(ref)
    iv[...] = iv_ref[...]
    ib[...] = ib_ref[...]
    for block, ref in enumerate((low_ref, centre_ref, high_ref)):
        rows = pl.ds(PAD + block * BX, BX)
        for f, (main, side) in enumerate(((cm, cs), (om, os_))):
            for q in range(4):
                packed = ref[32 + 4 * f + q]
                for j in range(4):
                    z = 4 * q + j
                    main[4 + z, rows, :] = ref[NZ * f + z]
                    edge = pltpu.roll(packed, -(16 + HY * j) % BY, 1)
                    side[4 + z, rows, :] = jnp.where((lane < 16) | (lane >= BY - 16), edge, 0.0)
    cur, old = run_steps(
        ROUND, (cm, cs), (om, os_), ((s0, s1), (b0, b1), (bz0, bz1), (bx0, bx1), (by0, by1)),
        fwd_ref, (iv, ib), place_ref, which_ref, count_ref, trace_ref, True,
    )
    rows = pl.ds(PAD + BX, BX)
    for z in range(NZ):
        now_ref[z] = cur[0][4 + z, rows, :]
        prev_ref[z] = old[0][4 + z, rows, :]
        images_ref[z // 2, z % 2] = iv[z]
        images_ref[z // 2, 2 + z % 2] = ib[z]


def shape(*dims, dtype=jnp.float32):
    return jax.ShapeDtypeStruct(dims, dtype)


PARAMS = pltpu.CompilerParams(vmem_limit_bytes=32 * 1024 * 1024)


def swap(x, axis, pairs):
    return lax.ppermute(x, axis, [(a, b) for a, b in pairs] + [(b, a) for a, b in pairs])


def shards(velocity, buoyancy, fwd_field, adjoint_now, adjoint_prev, recv_cell, traces):
    now, prev, fwd = adjoint_now[0], adjoint_prev[0], fwd_field[0]
    gx, gy, shot = lax.axis_index("gx"), lax.axis_index("gy"), lax.axis_index("shot")
    where = jnp.stack([gx * BX, gy * BY, gy % 2, shot % 2]).astype(jnp.int32)
    count_y, count_x = lax.axis_size("gy"), lax.axis_size("gx")

    place, which, count = pl.pallas_call(
        find_kernel,
        out_shape=(shape(RECV + 8, dtype=jnp.int32), shape(RECV + 8, dtype=jnp.int32), shape(1, dtype=jnp.int32)),
        in_specs=[SM, SM],
        out_specs=(SM, SM, SM),
        name="find_receivers",
    )(where, recv_cell[0])

    own = jnp.concatenate([velocity, buoyancy], axis=0)
    half = lax.all_to_all(
        jnp.broadcast_to(own, (4,) + own.shape), "shot", 0, 0, axis_index_groups=[[0, 2, 4, 6], [1, 3, 5, 7]]
    ).reshape(16, BX, BY)

    first, second = pl.pallas_call(
        pack_kernel,
        out_shape=(shape(12, BX, BY), shape(12, BX, BY)),
        in_specs=[SM, VM, VM, VM],
        out_specs=(VM, VM),
        name="pack_sides",
    )(where, now, prev, half)
    first = swap(first, "gy", [(i, i + 1) for i in range(0, count_y, 2)])
    second = swap(second, "gy", [(i, i + 1) for i in range(1, count_y - 1, 2)])

    up = [(i, i + 1) for i in range(count_x - 1)]
    down = [(b, a) for a, b in up]
    centre = jnp.concatenate([now, prev, half, first, second], axis=0)
    low = lax.ppermute(centre, "gx", up)
    high = lax.ppermute(centre, "gx", down)

    model = jnp.concatenate(
        [part for block in (centre, low, high) for part in (block[32:48], block[56:60], block[68:72])], axis=0
    )
    other = lax.ppermute(model, "shot", [(i, i ^ 1) for i in range(SHOTS)])

    ext = shape(NZ, EXT, BY)
    pad = shape(LAYERS, ROWS, BY)
    scratch = [pltpu.VMEM((LAYERS, ROWS, BY), jnp.float32)] * 4
    image = shape(NZ, BX, BY)
    outs = pl.pallas_call(
        first_kernel,
        out_shape=(shape(40, BX, BY), image, image, ext, ext, pad, pad) + (ext,) * 6,
        in_specs=[SM] * 5 + [VM] * 5,
        out_specs=(VM,) * 13,
        scratch_shapes=scratch,
        compiler_params=PARAMS,
        name="first_steps",
    )(where, place, which, count, traces[0], centre, low, high, other, fwd[:ROUND])
    send, iv, ib, coefs = outs[0], outs[1], outs[2], outs[3:]
    low = lax.ppermute(send, "gx", up)
    high = lax.ppermute(send, "gx", down)
    now, prev, images = pl.pallas_call(
        second_kernel,
        out_shape=(image, image, shape(SHOTS, 4, BX, BY)),
        in_specs=[SM] * 4 + [VM] * 16,
        out_specs=(VM,) * 3,
        scratch_shapes=scratch + [pltpu.VMEM((NZ, BX, BY), jnp.float32)] * 2,
        compiler_params=PARAMS,
        name="second_steps",
    )(place, which, count, traces[0], send, low, high, fwd[ROUND:], iv, ib, *coefs)
    parts = jnp.sum(lax.all_to_all(images, "shot", 0, 0), axis=0)
    scale = 1.0 / (SHOTS * STEPS) ** 0.5
    grad_vel = 2.0 * courant * velocity * parts[:2] * scale
    grad_buoy = courant * velocity * velocity * parts[2:] * scale
    return grad_vel, grad_buoy, now[None], prev[None]


def solution(mesh):
    return jax.shard_map(
        shards,
        mesh=mesh,
        in_specs=(
            P("shot", "gx", "gy"),
            P("shot", "gx", "gy"),
            P("shot", None, None, "gx", "gy"),
            P("shot", None, "gx", "gy"),
            P("shot", None, "gx", "gy"),
            P("shot", None),
            P("shot", None, None),
        ),
        out_specs=(
            P("shot", "gx", "gy"),
            P("shot", "gx", "gy"),
            P("shot", None, "gx", "gy"),
            P("shot", None, "gx", "gy"),
        ),
        check_vma=False,
    )
```

```python
import functools

import jax
import jax.numpy as jnp
from jax import lax
from jax.experimental import pallas as pl
from jax.experimental.pallas import tpu as pltpu
from jax.sharding import PartitionSpec as P

NZ, BX, BY = 16, 16, 128
FULL_X, FULL_Y = 256, 512
STEPS, SHOTS, RECV = 8, 8, 256
ROUND = 4
HY = 32
EXT = 3 * BX
PAD = 8
ROWS = EXT + 2 * PAD
LAYERS = NZ + 8
FAR = BY - HY
IMG = BX + 8

second_coef = (-205.0 / 72.0, 8.0 / 5.0, -1.0 / 5.0, 8.0 / 315.0, -1.0 / 560.0)
first_coef = (4.0 / 5.0, -1.0 / 5.0, 4.0 / 105.0, -1.0 / 280.0)
courant = 0.15
lap_unit = second_coef[4]
slope_unit = first_coef[3]
lap_ratio = (3.0 * second_coef[0] / lap_unit,) + tuple(c / lap_unit for c in second_coef[1:4])
slope_ratio = tuple(c / slope_unit for c in first_coef[:3])

VM = pl.BlockSpec(memory_space=pltpu.VMEM)
SM = pl.BlockSpec(memory_space=pltpu.SMEM)


def side_planes(groups):
    return NZ // groups + 8


def lane_of(rows):
    return lax.broadcasted_iota(jnp.int32, (rows, BY), 1)


def roll(x, shift):
    shift %= BY
    return pltpu.roll(x, shift, 1) if shift else x


def find_kernel(where_ref, recv_ref, place_ref, place4_ref, which_ref, count_ref):
    base_x = where_ref[0] - BX
    base_y = where_ref[1]

    def body(j, count):
        cell = recv_ref[j]
        z = lax.shift_right_logical(cell, 17)
        x = (lax.shift_right_logical(cell, 9) & (FULL_X - 1)) - base_x
        y = (cell & (FULL_Y - 1)) - base_y
        inside = (x >= 0) & (x < EXT) & (y >= -HY) & (y < BY + HY)
        main = (y >= 0) & (y < BY)
        right = y >= BY
        row = (x & 63) + PAD
        plane = jnp.where(main, z + 4, LAYERS + 4 + (z & 7))
        lane = jnp.where(main, y, lax.shift_right_logical(z, 3) * 64 + jnp.where(right, y - BY, y + 64))
        place_ref[count] = (plane * 64 + row) * 256 + (lane & 255)
        near = (y >= -16) & (y < BY + 16)
        plane = jnp.where(main, z + 4, LAYERS + 4 + (z & 3))
        lane = jnp.where(main, y, lax.shift_right_logical(z, 2) * 32 + jnp.where(right, y - BY, y + 32))
        lane = jnp.where(near, lane, 255)
        place4_ref[count] = (plane * 64 + row) * 256 + (lane & 255)
        which_ref[count] = j
        return count + inside.astype(jnp.int32)

    count_ref[0] = lax.fori_loop(0, RECV, body, jnp.int32(0))


def pack_kernel(where_ref, fields_ref, model_ref, first_ref, second_ref):
    even = where_ref[2] == 0
    lane = lane_of(BX)
    out = 0
    for ref in (fields_ref, model_ref):
        for base in range(0, ref.shape[0], NZ):
            for q in range(4):
                right = left = None
                for i in range(4):
                    plane = ref[base + q + 4 * i]
                    j = i ^ 1
                    a, b = roll(plane, HY * j - FAR), roll(plane, HY * i)
                    right = a if right is None else jnp.where((lane >= HY * j) & (lane < HY * (j + 1)), a, right)
                    left = b if left is None else jnp.where((lane >= HY * i) & (lane < HY * (i + 1)), b, left)
                first_ref[out] = jnp.where(even, right, left)
                second_ref[out] = jnp.where(even, left, right)
                out += 1


def side_pair(first, second, even, lane):
    right = jnp.where(even, first, second)
    left = jnp.where(even, second, first)
    is_right = (lane & 63) < HY
    return (
        jnp.where(is_right, right, left),
        jnp.where(is_right, roll(right, -HY), roll(left, HY)),
    )


def four_from_two(near, far, lane):
    inner = (lane & 31) < 16
    own = (lane & 63) < 32
    return jnp.where(
        inner, jnp.where(own, near, roll(far, 32)), jnp.where(own, roll(near, -32), far)
    )


def repeat_sides(ref, groups):
    per = NZ // groups
    w = BY // groups
    rows = pl.ds(PAD, EXT)
    lane = lane_of(EXT)
    at = LAYERS + 4
    for i in range(4):
        after = roll(ref[at + i, rows, :], -w)
        ref[at + per + i, rows, :] = jnp.where(lane < BY - w, after, 0.0)
        before = roll(ref[at + per - 4 + i, rows, :], w)
        ref[at - 4 + i, rows, :] = jnp.where(lane >= w, before, 0.0)


def clear_ends(ref):
    for z in (0, 1, 2, 3, NZ + 4, NZ + 5, NZ + 6, NZ + 7):
        ref[z] = jnp.zeros(ref.shape[1:], jnp.float32)


def clear(ref):
    def body(z, _):
        ref[z] = jnp.zeros(ref.shape[1:], jnp.float32)
        return 0

    lax.fori_loop(0, ref.shape[0], body, 0)


def derivs(ref, at, row, n, here, edges, lane, width, lap_too=True):
    inner = lane & (width - 1)
    lap = lap_ratio[0] * here if lap_too else None
    dz = dx = dy = None
    for k in (4, 3, 2, 1):
        up = roll(jnp.where(inner < k, edges, here), -k)
        down = roll(jnp.where(inner >= width - k, edges, here), k)
        zp = ref[at + k, pl.ds(row, n), :]
        zm = ref[at - k, pl.ds(row, n), :]
        xp = ref[at, pl.ds(row + k, n), :]
        xm = ref[at, pl.ds(row - k, n), :]
        if lap_too:
            both = ((zp + zm) + (xp + xm)) + (up + down)
            lap = lap + (both if k == 4 else lap_ratio[k] * both)
        if k == 4:
            dz, dx, dy = zp - zm, xp - xm, up - down
        else:
            c = slope_ratio[k - 1]
            dz, dx, dy = dz + c * (zp - zm), dx + c * (xp - xm), dy + c * (up - down)
    return lap, dz, dx, dy


def group_derivs(ref, p, lo, n, groups, sides=True, lap_too=True):
    per = NZ // groups
    w = BY // groups
    lane = lane_of(n)
    row = PAD + lo
    spot = pl.ds(row, n)
    side_at = LAYERS + 4 + p
    side = ref[side_at, spot, :]
    mains = [ref[4 + p + g * per, spot, :] for g in range(groups)]
    for g in range(groups):
        edges = jnp.where(lane < 64, roll(side, -g * w), roll(side, -(g + 1) * w))
        at = 4 + p + g * per
        yield 0, p + g * per, at, mains[g], derivs(ref, at, row, n, mains[g], edges, lane, BY, lap_too)
    if sides:
        edges = None
        for g in range(groups):
            first = roll(mains[(g - 1) % groups], g * w)
            last = roll(mains[(g + 1) % groups], (g + 1) * w)
            for start, value in ((g * w, first), (g * w + w // 2, last)):
                edges = value if edges is None else jnp.where(lane >= start, value, edges)
        yield 1, p, side_at, side, derivs(ref, side_at, row, n, side, edges, lane, w, lap_too)


PLANS = ((4, 12, 20, 28, 36), (8, 16, 24, 32), (12, 20, 28), (16, 24))


def run_steps(first_step, groups, cur, old, coefs, fwd_ref, image, place_ref, which_ref, count_ref, trace_ref, last):
    lane1 = lane_of(1)
    for j, plan in enumerate(PLANS):

        def add(i, _, cur=cur, step=first_step + j):
            place = place_ref[i]
            value = trace_ref[step, which_ref[i]]
            spot = (lax.shift_right_logical(place, 14), pl.ds(lax.shift_right_logical(place, 8) & 63, 1), slice(None))
            cur[spot] = cur[spot] + jnp.where(lane1 == (place & 255), value, 0.0)
            return 0

        lax.fori_loop(0, count_ref[0], add, 0)
        repeat_sides(cur, groups)
        sides = not (last and j == ROUND - 1)

        def layers(p, _, cur=cur, old=old, plan=plan, j=j, sides=sides):
            for lo in plan:
                rows = pl.ds(lo, 8)
                for kind, z, at, here, found in group_derivs(cur, p, lo, 8, groups, sides):
                    terms = [coefs[c][kind][z, rows, :] * found[c] for c in range(4)]
                    change = (terms[0] + terms[1]) + (terms[2] + terms[3])
                    spot = (at, pl.ds(PAD + lo, 8), slice(None))
                    old[spot] = ((here + here) - old[spot]) + change
                    if kind == 0 and BX - 8 < lo < 2 * BX:
                        seen = pl.ds(lo - (BX - 4), 8)
                        snapshot = fwd_ref[j, z, seen, :]
                        image[0][z, seen, :] += snapshot * change
                        image[1][z, seen, :] += snapshot * found[0]
            return 0

        lax.fori_loop(0, NZ // groups, layers, 0)
        cur, old = old, cur
    return cur, old


def widen(fwd_ref, wide_ref):
    for step in range(ROUND):

        def body(z, _, step=step):
            wide_ref[step, z, pl.ds(4, BX), :] = fwd_ref[step, z].astype(jnp.float32)
            return 0

        lax.fori_loop(0, NZ, body, 0, unroll=4)


def first_kernel(
    where_ref, place_ref, which_ref, count_ref, trace_ref,
    centre_ref, low_ref, high_ref, centre_fields, low_fields, high_fields, other_ref, fwd_ref,
    send_ref, iv_ref, ib_ref, m0, m1, m2, m3, f0, f1, f2, f3,
    cur, old, buoy, speed, speed_side, t0, t1, t2, t3, wide,
):
    even = where_ref[2] == 0
    core = where_ref[3]
    lane = lane_of(BX)
    for ref in (cur, old, buoy):
        clear_ends(ref)
    clear(iv_ref)
    clear(ib_ref)
    widen(fwd_ref, wide)
    at = LAYERS + 4
    blocks = ((low_ref, low_fields), (centre_ref, centre_fields), (high_ref, high_fields))
    for block, (ref, fields) in enumerate(blocks):
        rows = pl.ds(PAD + block * BX, BX)
        bare = pl.ds(block * BX, BX)
        for f, field in enumerate((cur, old)):
            for z in range(NZ):
                field[4 + z, rows, :] = fields[NZ * f + z]
            for q in range(4):
                near, far = side_pair(ref[16 + 4 * f + q], ref[28 + 4 * f + q], even, lane)
                field[at + q, rows, :] = near
                field[at + q + 4, rows, :] = far
        for half in (0, 1):
            turn = core if half == 0 else 1 - core
            spot = (1, 0, 2)[block]
            for t in range(4):
                z = 2 * turn + t % 2
                if half == 0:
                    planes = [ref[4 * i + t] for i in range(4)]
                    packs = ref[24 + t], ref[36 + t]
                else:
                    planes = [other_ref[24 * spot + 4 * i + t] for i in range(4)]
                    packs = other_ref[24 * spot + 16 + t], other_ref[24 * spot + 20 + t]
                pair = side_pair(*packs, even, lane)
                if t < 2:
                    for i in range(4):
                        speed[z + 4 * i, bare, :] = courant * planes[i] * planes[i]
                    for i in range(2):
                        speed_side[z + 4 * i, bare, :] = courant * pair[i] * pair[i]
                else:
                    for i in range(4):
                        buoy[4 + z + 4 * i, rows, :] = planes[i]
                    for i in range(2):
                        buoy[at + z + 4 * i, rows, :] = pair[i]
    repeat_sides(buoy, 2)
    coefs = ((m0, t0), (m1, t1), (m2, t2), (m3, t3))

    def slopes(p, _):
        for lo in PLANS[0]:
            rows = pl.ds(lo, 8)
            for kind, z, _, here, found in group_derivs(buoy, p, lo, 8, 2, lap_too=False):
                pace = (speed, speed_side)[kind][z, rows, :]
                coefs[0][kind][z, rows, :] = (lap_unit * pace) * here
                steep = (slope_unit * slope_unit) * pace
                for c in (1, 2, 3):
                    coefs[c][kind][z, rows, :] = steep * found[c]
        return 0

    lax.fori_loop(0, NZ // 2, slopes, 0)
    lane8 = lane_of(8)
    for wide_side, side in ((t0, f0), (t1, f1), (t2, f2), (t3, f3)):
        for p in range(4):
            for lo in PLANS[0]:
                rows = pl.ds(lo, 8)
                side[p, rows, :] = four_from_two(wide_side[p, rows, :], wide_side[p + 4, rows, :], lane8)
    now, prev = run_steps(
        0, 2, cur, old, coefs, wide, (iv_ref, ib_ref), place_ref, which_ref, count_ref, trace_ref, False
    )
    rows = pl.ds(PAD + BX, BX)
    for f, field in enumerate((now, prev)):
        for z in range(NZ):
            send_ref[NZ * f + z] = field[4 + z, rows, :]
        for p in range(4):
            send_ref[2 * NZ + 4 * f + p] = four_from_two(field[at + p, rows, :], field[at + p + 4, rows, :], lane)


def second_kernel(
    place_ref, which_ref, count_ref, trace_ref,
    centre_ref, low_ref, high_ref, fwd_ref, iv_ref, ib_ref, m0, m1, m2, m3, f0, f1, f2, f3,
    now_ref, prev_ref, images_ref,
    cur, old, iv, ib, wide,
):
    for ref in (cur, old):
        clear_ends(ref)
    clear(iv)
    clear(ib)
    widen(fwd_ref, wide)
    at = LAYERS + 4
    for block, ref in enumerate((low_ref, centre_ref, high_ref)):
        rows = pl.ds(PAD + block * BX, BX)
        for f, field in enumerate((cur, old)):
            for z in range(NZ):
                field[4 + z, rows, :] = ref[NZ * f + z]
            for p in range(4):
                field[at + p, rows, :] = ref[2 * NZ + 4 * f + p]
    now, prev = run_steps(
        ROUND, 4, cur, old, ((m0, f0), (m1, f1), (m2, f2), (m3, f3)), wide, (iv, ib),
        place_ref, which_ref, count_ref, trace_ref, True,
    )
    rows = pl.ds(PAD + BX, BX)
    wanted = pl.ds(4, BX)
    for z in range(NZ):
        now_ref[z] = now[4 + z, rows, :]
        prev_ref[z] = prev[4 + z, rows, :]
        images_ref[z // 2, z % 2] = iv[z, wanted, :] + iv_ref[z, wanted, :]
        images_ref[z // 2, 2 + z % 2] = ib[z, wanted, :] + ib_ref[z, wanted, :]


def shape(*dims, dtype=jnp.float32):
    return jax.ShapeDtypeStruct(dims, dtype)


def room(mib):
    return pltpu.CompilerParams(vmem_limit_bytes=mib * 1024 * 1024)


PARAMS = room(32)


def buffer(*dims):
    return pltpu.VMEM(dims, jnp.float32)


def steps_one(*operands):
    ext, side_ext = shape(NZ, EXT, BY), shape(NZ // 4, EXT, BY)
    image = shape(NZ, IMG, BY)
    block = LAYERS + side_planes(2)
    return pl.pallas_call(
        first_kernel,
        out_shape=(shape(40, BX, BY), image, image) + (ext,) * 4 + (side_ext,) * 4,
        in_specs=[SM] * 5 + [VM] * 8,
        out_specs=(VM,) * 11,
        scratch_shapes=[buffer(block, ROWS, BY)] * 3
        + [buffer(NZ, EXT, BY)]
        + [buffer(NZ // 2, EXT, BY)] * 5
        + [buffer(ROUND, NZ, IMG, BY)],
        compiler_params=PARAMS,
        name="first_steps",
    )(*operands)


def steps_two(*operands):
    block = LAYERS + side_planes(4)
    return pl.pallas_call(
        second_kernel,
        out_shape=(shape(NZ, BX, BY), shape(NZ, BX, BY), shape(SHOTS, 4, BX, BY)),
        in_specs=[SM] * 4 + [VM] * 14,
        out_specs=(VM,) * 3,
        scratch_shapes=[buffer(block, ROWS, BY)] * 2 + [buffer(NZ, IMG, BY)] * 2 + [buffer(ROUND, NZ, IMG, BY)],
        compiler_params=PARAMS,
        name="second_steps",
    )(*operands)


def swap(x, axis, pairs):
    return lax.ppermute(x, axis, [(a, b) for a, b in pairs] + [(b, a) for a, b in pairs])


def shards(velocity, buoyancy, fwd_field, adjoint_now, adjoint_prev, recv_cell, traces):
    now, prev, fwd = adjoint_now[0], adjoint_prev[0], fwd_field[0]
    gx, gy, shot = lax.axis_index("gx"), lax.axis_index("gy"), lax.axis_index("shot")
    where = jnp.stack([gx * BX, gy * BY, gy % 2, shot % 2]).astype(jnp.int32)
    count_y, count_x = lax.axis_size("gy"), lax.axis_size("gx")

    listed = shape(RECV + 8, dtype=jnp.int32)
    place, place4, which, count = pl.pallas_call(
        find_kernel,
        out_shape=(listed, listed, listed, shape(1, dtype=jnp.int32)),
        in_specs=[SM, SM],
        out_specs=(SM,) * 4,
        compiler_params=room(4),
        cost_estimate=pl.CostEstimate(flops=8000, bytes_accessed=4000, transcendentals=0),
        name="find_receivers",
    )(where, recv_cell[0])

    up = [(i, i + 1) for i in range(count_x - 1)]
    down = [(b, a) for a, b in up]
    fields = jnp.concatenate([now, prev], axis=0)
    low_fields = lax.ppermute(fields, "gx", up)
    high_fields = lax.ppermute(fields, "gx", down)

    own = jnp.concatenate([jnp.broadcast_to(part, (4,) + part.shape) for part in (velocity, buoyancy)], axis=1)
    half = lax.all_to_all(own, "shot", 0, 0, axis_index_groups=[[0, 2, 4, 6], [1, 3, 5, 7]]).reshape(16, BX, BY)

    first, second = pl.pallas_call(
        pack_kernel,
        out_shape=(shape(12, BX, BY), shape(12, BX, BY)),
        in_specs=[SM, VM, VM],
        out_specs=(VM, VM),
        compiler_params=room(8),
        name="pack_sides",
    )(where, fields, half)
    first = swap(first, "gy", [(i, i + 1) for i in range(0, count_y, 2)])
    second = swap(second, "gy", [(i, i + 1) for i in range(1, count_y - 1, 2)])

    centre = jnp.concatenate([half, first, second], axis=0)
    centre, low_fields, high_fields, place, place4, which, count = lax.optimization_barrier(
        (centre, low_fields, high_fields, place, place4, which, count)
    )
    low = lax.ppermute(centre, "gx", up)
    high = lax.ppermute(centre, "gx", down)

    model = jnp.concatenate(
        [part for block in (centre, low, high) for part in (block[0:16], block[24:28], block[36:40])], axis=0
    )
    other = lax.ppermute(model, "shot", [(i, i ^ 1) for i in range(SHOTS)])

    outs = steps_one(
        where, place, which, count, traces[0], centre, low, high, fields, low_fields, high_fields, other, fwd[:ROUND]
    )
    send, iv, ib, coefs = outs[0], outs[1], outs[2], outs[3:]
    low = lax.ppermute(send, "gx", up)
    high = lax.ppermute(send, "gx", down)
    now, prev, images = steps_two(place4, which, count, traces[0], send, low, high, fwd[ROUND:], iv, ib, *coefs)
    parts = jnp.sum(lax.all_to_all(images, "shot", 0, 0), axis=0)
    scale = 1.0 / (SHOTS * STEPS) ** 0.5
    grad_vel = 2.0 * parts[:2] / velocity * scale
    grad_buoy = courant * velocity * velocity * (lap_unit * parts[2:]) * scale
    return grad_vel, grad_buoy, now[None], prev[None]


def solution(mesh):
    return jax.shard_map(
        shards,
        mesh=mesh,
        in_specs=(
            P("shot", "gx", "gy"),
            P("shot", "gx", "gy"),
            P("shot", None, None, "gx", "gy"),
            P("shot", None, "gx", "gy"),
            P("shot", None, "gx", "gy"),
            P("shot", None),
            P("shot", None, None),
        ),
        out_specs=(
            P("shot", "gx", "gy"),
            P("shot", "gx", "gy"),
            P("shot", None, "gx", "gy"),
            P("shot", None, "gx", "gy"),
        ),
        check_vma=False,
    )
```

```python
import functools

import jax
import jax.numpy as jnp
import numpy as np
from jax import lax
from jax.experimental import pallas as pl
from jax.experimental.pallas import tpu as pltpu
from jax.sharding import PartitionSpec as P

NZ, BX, BY = 16, 16, 128
FULL_X, FULL_Y = 256, 512
STEPS, SHOTS, RECV = 8, 8, 256
ROUND = 4
HY = 32
EXT = 3 * BX
PAD = 8
ROWS = EXT + 2 * PAD
LAYERS = NZ + 8
FAR = BY - HY
IMG = BX + 8

second_coef = (-205.0 / 72.0, 8.0 / 5.0, -1.0 / 5.0, 8.0 / 315.0, -1.0 / 560.0)
first_coef = (4.0 / 5.0, -1.0 / 5.0, 4.0 / 105.0, -1.0 / 280.0)
courant = 0.15
lap_unit = second_coef[4]
slope_unit = first_coef[3]
lap_ratio = (3.0 * second_coef[0] / lap_unit,) + tuple(c / lap_unit for c in second_coef[1:4])
slope_ratio = tuple(c / slope_unit for c in first_coef[:3])

VM = pl.BlockSpec(memory_space=pltpu.VMEM)
SM = pl.BlockSpec(memory_space=pltpu.SMEM)


def side_planes(groups):
    return NZ // groups + 8


def lane_of(rows):
    return lax.broadcasted_iota(jnp.int32, (rows, BY), 1)


def roll(x, shift):
    shift %= BY
    return pltpu.roll(x, shift, 1) if shift else x


def find_kernel(where_ref, recv_ref, place_ref, place4_ref, which_ref, count_ref):
    base_x = where_ref[0] - BX
    base_y = where_ref[1]

    def body(j, count):
        cell = recv_ref[j]
        z = lax.shift_right_logical(cell, 17)
        x = (lax.shift_right_logical(cell, 9) & (FULL_X - 1)) - base_x
        y = (cell & (FULL_Y - 1)) - base_y
        inside = (x >= 0) & (x < EXT) & (y >= -HY) & (y < BY + HY)
        main = (y >= 0) & (y < BY)
        right = y >= BY
        row = (x & 63) + PAD
        plane = jnp.where(main, z + 4, LAYERS + 4 + (z & 7))
        lane = jnp.where(main, y, lax.shift_right_logical(z, 3) * 64 + jnp.where(right, y - BY, y + 64))
        place_ref[count] = (plane * 64 + row) * 256 + (lane & 255)
        near = (y >= -16) & (y < BY + 16)
        plane = jnp.where(main, z + 4, LAYERS + 4 + (z & 3))
        lane = jnp.where(main, y, lax.shift_right_logical(z, 2) * 32 + jnp.where(right, y - BY, y + 32))
        lane = jnp.where(near, lane, 255)
        place4_ref[count] = (plane * 64 + row) * 256 + (lane & 255)
        which_ref[count] = j
        return count + inside.astype(jnp.int32)

    count_ref[0] = lax.fori_loop(0, RECV, body, jnp.int32(0), unroll=4)


def pack_kernel(where_ref, fields_ref, model_ref, first_ref, second_ref):
    even = where_ref[2] == 0
    lane = lane_of(BX)
    out = 0
    for ref in (fields_ref, model_ref):
        for base in range(0, ref.shape[0], NZ):
            for q in range(4):
                right = left = None
                for i in range(4):
                    plane = ref[base + q + 4 * i]
                    j = i ^ 1
                    a, b = roll(plane, HY * j - FAR), roll(plane, HY * i)
                    right = a if right is None else jnp.where((lane >= HY * j) & (lane < HY * (j + 1)), a, right)
                    left = b if left is None else jnp.where((lane >= HY * i) & (lane < HY * (i + 1)), b, left)
                first_ref[out] = jnp.where(even, right, left)
                second_ref[out] = jnp.where(even, left, right)
                out += 1


def side_pair(first, second, even, lane):
    right = jnp.where(even, first, second)
    left = jnp.where(even, second, first)
    is_right = (lane & 63) < HY
    return (
        jnp.where(is_right, right, left),
        jnp.where(is_right, roll(right, -HY), roll(left, HY)),
    )


def four_from_two(near, far, lane):
    inner = (lane & 31) < 16
    own = (lane & 63) < 32
    return jnp.where(
        inner, jnp.where(own, near, roll(far, 32)), jnp.where(own, roll(near, -32), far)
    )


def repeat_sides(ref, groups):
    per = NZ // groups
    w = BY // groups
    rows = pl.ds(PAD, EXT)
    lane = lane_of(EXT)
    at = LAYERS + 4
    for i in range(4):
        after = roll(ref[at + i, rows, :], -w)
        ref[at + per + i, rows, :] = jnp.where(lane < BY - w, after, 0.0)
        before = roll(ref[at + per - 4 + i, rows, :], w)
        ref[at - 4 + i, rows, :] = jnp.where(lane >= w, before, 0.0)


def clear_ends(ref):
    for z in (0, 1, 2, 3, NZ + 4, NZ + 5, NZ + 6, NZ + 7):
        ref[z] = jnp.zeros(ref.shape[1:], jnp.float32)


PARTS = 3


def side_columns(groups):
    w = BY // groups
    lane = np.arange(BY)
    t = lane % w
    return lane // w, np.where(t < w // 2, BY + t, t - w)


def shift_weights(group_to, y_to, group_from, y_from):
    lap_k = np.array((0, 8064, -1008, 128, -9) + (0,) * 4, np.float32)
    slope_k = np.array((0, 672, -168, 32, -3) + (0,) * 4, np.float32)
    away = y_from[:, None] - y_to[None, :]
    k = np.where((group_from[:, None] == group_to[None, :]) & (abs(away) < 5), abs(away), 0)
    return np.concatenate([lap_k[k], slope_k[k] * np.sign(away)], axis=1)


def layer_weights(groups):
    side_group, side_y = side_columns(groups)
    y = np.arange(BY)
    both = []
    for g in range(groups):
        own = np.full(BY, g)
        both.append(np.concatenate([shift_weights(own, y, own, y), shift_weights(own, y, side_group, side_y)], axis=0))
    return jnp.asarray(np.stack(both), jnp.bfloat16)


def side_weights(groups):
    side_group, side_y = side_columns(groups)
    y = np.arange(BY)
    rows = [shift_weights(side_group, side_y, side_group, side_y)]
    rows += [shift_weights(side_group, side_y, np.full(BY, g), y) for g in range(groups)]
    return jnp.asarray(np.concatenate(rows, axis=0), jnp.bfloat16)


def shift_along_y(ref, groups, start, n, work, sides=True, lap_too=True):
    cut_layers, cut_sides, layer_w, side_w, y_lap, y_slope = work
    per = NZ // groups
    rows = pl.ds(PAD + start, n)

    def cut(at, to, z):
        x = ref[at, rows, :]
        for part in range(PARTS):
            piece = x.astype(jnp.bfloat16)
            to[part, z, pl.ds(0, n), :] = piece
            x = x - piece.astype(jnp.float32)

    def cut_group(p, _):
        for g in range(groups):
            cut(4 + p + g * per, cut_layers, p + g * per)
        cut(LAYERS + 4 + p, cut_sides, p)
        return 0

    lax.fori_loop(0, per, cut_group, 0, unroll=True)
    if sides:
        repeat_sides(ref, groups)

    def product(pieces, weights, first):
        weights = weights if lap_too else weights[:, BY:]
        found = jnp.dot(
            jnp.concatenate(pieces, axis=1), jnp.concatenate([weights] * PARTS, axis=0), preferred_element_type=jnp.float32
        )
        if lap_too:
            y_lap[first : first + per, pl.ds(start, n), :] = found[:, :BY].reshape(per, n, BY)
        y_slope[first : first + per, pl.ds(start, n), :] = found[:, -BY:].reshape(per, n, BY)

    def layer_piece(part, g):
        return cut_layers[part, g * per : (g + 1) * per, pl.ds(0, n), :].reshape(per * n, BY)

    def side_piece(part):
        return cut_sides[part, :, pl.ds(0, n), :].reshape(per * n, BY)

    for g in range(groups):
        pieces = [x for part in range(PARTS) for x in (layer_piece(part, g), side_piece(part))]
        product(pieces, layer_w[g], g * per)
    if sides:
        pieces = []
        for part in range(PARTS):
            pieces += [side_piece(part)] + [layer_piece(part, g) for g in range(groups)]
        product(pieces, side_w[...], NZ)


def along_zx(ref, at, row, n, lap_too=True):
    lap = dz = dx = None
    for k in (4, 3, 2, 1):
        zp = ref[at + k, pl.ds(row, n), :]
        zm = ref[at - k, pl.ds(row, n), :]
        xp = ref[at, pl.ds(row + k, n), :]
        xm = ref[at, pl.ds(row - k, n), :]
        if lap_too:
            both = (zp + zm) + (xp + xm)
            lap = both if k == 4 else lap + lap_ratio[k] * both
        c = slope_ratio[k - 1] if k < 4 else None
        dz = zp - zm if k == 4 else dz + c * (zp - zm)
        dx = xp - xm if k == 4 else dx + c * (xp - xm)
    return lap, dz, dx


def group_places(p, groups, sides=True):
    per = NZ // groups
    places = [(0, p + g * per, 4 + p + g * per, p + g * per) for g in range(groups)]
    return places + [(1, p, LAYERS + 4 + p, NZ + p)] * sides


PLANS = ((4, 12, 20, 28, 36), (8, 16, 24, 32), (12, 20, 28), (16, 24))
WINDOWS = ((0, 48), (8, 32), (8, 32), (16, 16))


def run_steps(first_step, groups, cur, old, coefs, fwd_ref, image, place_ref, which_ref, count_ref, trace_ref, work, last):
    lane1 = lane_of(1)
    y_lap, y_slope = work[-2:]
    for j, plan in enumerate(PLANS):

        def add(i, _, cur=cur, step=first_step + j):
            place = place_ref[i]
            value = trace_ref[step, which_ref[i]]
            spot = (lax.shift_right_logical(place, 14), pl.ds(lax.shift_right_logical(place, 8) & 63, 1), slice(None))
            cur[spot] = cur[spot] + jnp.where(lane1 == (place & 255), value, 0.0)
            return 0

        lax.fori_loop(0, count_ref[0], add, 0)
        sides = not (last and j == ROUND - 1)
        shift_along_y(cur, groups, *WINDOWS[j], work, sides)

        def layers(p, _, cur=cur, old=old, plan=plan, j=j, sides=sides):
            for lo in plan:
                rows = pl.ds(lo, 8)
                for kind, z, at, y in group_places(p, groups, sides):
                    lap, dz, dx = along_zx(cur, at, PAD + lo, 8)
                    spot = (at, pl.ds(PAD + lo, 8), slice(None))
                    here = cur[spot]
                    lap = (lap + (-1.0 / 9.0) * y_lap[y, rows, :]) + lap_ratio[0] * here
                    found = lap, dz, dx, y_slope[y, rows, :]
                    terms = [coefs[c][kind][z, rows, :] * found[c] for c in range(4)]
                    change = (terms[0] + terms[1]) + (terms[2] + terms[3])
                    old[spot] = ((here + here) - old[spot]) + change
                    if kind == 0 and BX - 8 < lo < 2 * BX:
                        seen = pl.ds(lo - (BX - 4), 8)
                        snapshot = fwd_ref[j, z, seen, :]
                        for total, term in zip(image, (snapshot * change, snapshot * lap)):
                            total[z, seen, :] = total[z, seen, :] + term if j else term
            return 0

        lax.fori_loop(0, NZ // groups, layers, 0)
        cur, old = old, cur
    return cur, old


def widen(fwd_ref, wide_ref):
    for step in range(ROUND):

        def body(z, _, step=step):
            wide_ref[step, z, pl.ds(4, BX), :] = fwd_ref[step, z].astype(jnp.float32)
            return 0

        lax.fori_loop(0, NZ, body, 0, unroll=4)


def first_kernel(
    where_ref, place_ref, which_ref, count_ref, trace_ref,
    centre_ref, low_ref, high_ref, centre_fields, low_fields, high_fields, other_ref, fwd_ref, layer_w, side_w,
    send_ref, iv_ref, ib_ref, m0, m1, m2, m3, f0, f1, f2, f3,
    cur, old, buoy, speed, speed_side, t0, t1, t2, t3, wide, cut_layers, cut_sides, y_lap, y_slope,
):
    work = cut_layers, cut_sides, layer_w, side_w, y_lap, y_slope
    even = where_ref[2] == 0
    core = where_ref[3]
    lane = lane_of(BX)
    for ref in (cur, old, buoy):
        clear_ends(ref)
    widen(fwd_ref, wide)
    at = LAYERS + 4
    blocks = ((low_ref, low_fields), (centre_ref, centre_fields), (high_ref, high_fields))
    for block, (ref, fields) in enumerate(blocks):
        rows = pl.ds(PAD + block * BX, BX)
        bare = pl.ds(block * BX, BX)
        for f, field in enumerate((cur, old)):
            for z in range(NZ):
                field[4 + z, rows, :] = fields[NZ * f + z]
            for q in range(4):
                near, far = side_pair(ref[16 + 4 * f + q], ref[28 + 4 * f + q], even, lane)
                field[at + q, rows, :] = near
                field[at + q + 4, rows, :] = far
        for half in (0, 1):
            turn = core if half == 0 else 1 - core
            spot = (1, 0, 2)[block]
            for t in range(4):
                z = 2 * turn + t % 2
                if half == 0:
                    planes = [ref[4 * i + t] for i in range(4)]
                    packs = ref[24 + t], ref[36 + t]
                else:
                    planes = [other_ref[24 * spot + 4 * i + t] for i in range(4)]
                    packs = other_ref[24 * spot + 16 + t], other_ref[24 * spot + 20 + t]
                pair = side_pair(*packs, even, lane)
                if t < 2:
                    for i in range(4):
                        speed[z + 4 * i, bare, :] = courant * planes[i] * planes[i]
                    for i in range(2):
                        speed_side[z + 4 * i, bare, :] = courant * pair[i] * pair[i]
                else:
                    for i in range(4):
                        buoy[4 + z + 4 * i, rows, :] = planes[i]
                    for i in range(2):
                        buoy[at + z + 4 * i, rows, :] = pair[i]
    coefs = ((m0, t0), (m1, t1), (m2, t2), (m3, t3))

    shift_along_y(buoy, 2, 0, EXT, work, lap_too=False)

    def slopes(p, _):
        for lo in PLANS[0]:
            rows = pl.ds(lo, 8)
            for kind, z, at, y in group_places(p, 2):
                _lap, dz, dx = along_zx(buoy, at, PAD + lo, 8, lap_too=False)
                pace = (speed, speed_side)[kind][z, rows, :]
                coefs[0][kind][z, rows, :] = (lap_unit * pace) * buoy[at, pl.ds(PAD + lo, 8), :]
                steep = (slope_unit * slope_unit) * pace
                coefs[1][kind][z, rows, :] = steep * dz
                coefs[2][kind][z, rows, :] = steep * dx
                coefs[3][kind][z, rows, :] = ((1.0 / 840.0 / 840.0) * pace) * y_slope[y, rows, :]
        return 0

    lax.fori_loop(0, NZ // 2, slopes, 0)
    lane8 = lane_of(8)
    for wide_side, side in ((t0, f0), (t1, f1), (t2, f2), (t3, f3)):
        for p in range(4):
            for lo in PLANS[0]:
                rows = pl.ds(lo, 8)
                side[p, rows, :] = four_from_two(wide_side[p, rows, :], wide_side[p + 4, rows, :], lane8)
    now, prev = run_steps(
        0, 2, cur, old, coefs, wide, (iv_ref, ib_ref), place_ref, which_ref, count_ref, trace_ref, work, False
    )
    rows = pl.ds(PAD + BX, BX)
    for f, field in enumerate((now, prev)):
        for z in range(NZ):
            send_ref[NZ * f + z] = field[4 + z, rows, :]
        for p in range(4):
            send_ref[2 * NZ + 4 * f + p] = four_from_two(field[at + p, rows, :], field[at + p + 4, rows, :], lane)


def second_kernel(
    where_ref, place_ref, which_ref, count_ref, trace_ref,
    centre_ref, low_ref, high_ref, fwd_ref, iv_ref, ib_ref, m0, m1, m2, m3, f0, f1, f2, f3, layer_w, side_w,
    now_ref, prev_ref, keep_ref, give_ref,
    cur, old, iv, ib, wide, cut_layers, cut_sides, y_lap, y_slope,
):
    work = cut_layers, cut_sides, layer_w, side_w, y_lap, y_slope
    for ref in (cur, old):
        clear_ends(ref)
    widen(fwd_ref, wide)
    at = LAYERS + 4
    for block, ref in enumerate((low_ref, centre_ref, high_ref)):
        rows = pl.ds(PAD + block * BX, BX)
        for f, field in enumerate((cur, old)):
            for z in range(NZ):
                field[4 + z, rows, :] = ref[NZ * f + z]
            for p in range(4):
                field[at + p, rows, :] = ref[2 * NZ + 4 * f + p]
    now, prev = run_steps(
        ROUND, 4, cur, old, ((m0, f0), (m1, f1), (m2, f2), (m3, f3)), wide, (iv, ib),
        place_ref, which_ref, count_ref, trace_ref, work, True,
    )
    rows = pl.ds(PAD + BX, BX)
    wanted = pl.ds(4, BX)
    core = where_ref[3]
    for z in range(NZ):
        now_ref[z] = now[4 + z, rows, :]
        prev_ref[z] = prev[4 + z, rows, :]
    for i in range(4):
        for ref, turn in ((keep_ref, core), (give_ref, 1 - core)):
            for v in (0, 1):
                z = 4 * i + 2 * turn + v
                ref[i, v] = iv[z, wanted, :] + iv_ref[z, wanted, :]
                ref[i, 2 + v] = ib[z, wanted, :] + ib_ref[z, wanted, :]


def shape(*dims, dtype=jnp.float32):
    return jax.ShapeDtypeStruct(dims, dtype)


def room(mib):
    return pltpu.CompilerParams(vmem_limit_bytes=mib * 1024 * 1024)


PARAMS = room(32)


def buffer(*dims):
    return pltpu.VMEM(dims, jnp.float32)


def work_buffers(groups):
    planes = NZ + NZ // groups
    return [
        pltpu.VMEM((PARTS, NZ, EXT, BY), jnp.bfloat16),
        pltpu.VMEM((PARTS, NZ // groups, EXT, BY), jnp.bfloat16),
        buffer(planes, EXT, BY),
        buffer(planes, EXT, BY),
    ]


def steps_one(*operands):
    ext, side_ext = shape(NZ, EXT, BY), shape(NZ // 4, EXT, BY)
    image = shape(NZ, IMG, BY)
    block = LAYERS + side_planes(2)
    return pl.pallas_call(
        first_kernel,
        out_shape=(shape(40, BX, BY), image, image) + (ext,) * 4 + (side_ext,) * 4,
        in_specs=[SM] * 5 + [VM] * 10,
        out_specs=(VM,) * 11,
        scratch_shapes=[buffer(block, ROWS, BY)] * 3
        + [buffer(NZ, EXT, BY)]
        + [buffer(NZ // 2, EXT, BY)] * 5
        + [buffer(ROUND, NZ, IMG, BY)]
        + work_buffers(2),
        compiler_params=PARAMS,
        name="first_steps",
    )(*operands, layer_weights(2), side_weights(2))


def steps_two(*operands):
    block = LAYERS + side_planes(4)
    return pl.pallas_call(
        second_kernel,
        out_shape=(shape(NZ, BX, BY),) * 2 + (shape(4, 4, BX, BY),) * 2,
        in_specs=[SM] * 5 + [VM] * 16,
        out_specs=(VM,) * 4,
        scratch_shapes=[buffer(block, ROWS, BY)] * 2 + [buffer(NZ, IMG, BY)] * 2
        + [buffer(ROUND, NZ, IMG, BY)]
        + work_buffers(4),
        compiler_params=PARAMS,
        name="second_steps",
    )(*operands, layer_weights(4), side_weights(4))


def swap(x, axis, pairs):
    return lax.ppermute(x, axis, [(a, b) for a, b in pairs] + [(b, a) for a, b in pairs])


def shards(velocity, buoyancy, fwd_field, adjoint_now, adjoint_prev, recv_cell, traces):
    now, prev, fwd = adjoint_now[0], adjoint_prev[0], fwd_field[0]
    gx, gy, shot = lax.axis_index("gx"), lax.axis_index("gy"), lax.axis_index("shot")
    where = jnp.stack([gx * BX, gy * BY, gy % 2, shot % 2]).astype(jnp.int32)
    same_core = [list(range(core, SHOTS, 2)) for core in (0, 1)]
    other_core = [(i, i ^ 1) for i in range(SHOTS)]
    count_y, count_x = lax.axis_size("gy"), lax.axis_size("gx")

    listed = shape(RECV + 8, dtype=jnp.int32)
    place, place4, which, count = pl.pallas_call(
        find_kernel,
        out_shape=(listed, listed, listed, shape(1, dtype=jnp.int32)),
        in_specs=[SM, SM],
        out_specs=(SM,) * 4,
        compiler_params=room(4),
        cost_estimate=pl.CostEstimate(flops=8000, bytes_accessed=4000, transcendentals=0),
        name="find_receivers",
    )(where, recv_cell[0])

    up = [(i, i + 1) for i in range(count_x - 1)]
    down = [(b, a) for a, b in up]
    fields = jnp.concatenate([now, prev], axis=0)
    low_fields = lax.ppermute(fields, "gx", up)
    high_fields = lax.ppermute(fields, "gx", down)

    own = jnp.concatenate([jnp.broadcast_to(part, (4,) + part.shape) for part in (velocity, buoyancy)], axis=1)
    half = lax.all_to_all(own, "shot", 0, 0, axis_index_groups=same_core).reshape(16, BX, BY)

    first, second = pl.pallas_call(
        pack_kernel,
        out_shape=(shape(12, BX, BY), shape(12, BX, BY)),
        in_specs=[SM, VM, VM],
        out_specs=(VM, VM),
        compiler_params=room(8),
        name="pack_sides",
    )(where, fields, half)
    first = swap(first, "gy", [(i, i + 1) for i in range(0, count_y, 2)])
    second = swap(second, "gy", [(i, i + 1) for i in range(1, count_y - 1, 2)])

    centre = jnp.concatenate([half, first, second], axis=0)
    centre, low_fields, high_fields, place, place4, which, count = lax.optimization_barrier(
        (centre, low_fields, high_fields, place, place4, which, count)
    )
    low = lax.ppermute(centre, "gx", up)
    high = lax.ppermute(centre, "gx", down)

    model = jnp.concatenate(
        [part for block in (centre, low, high) for part in (block[0:16], block[24:28], block[36:40])], axis=0
    )
    other = lax.ppermute(model, "shot", other_core)

    outs = steps_one(
        where, place, which, count, traces[0], centre, low, high, fields, low_fields, high_fields, other, fwd[:ROUND]
    )
    send, iv, ib, coefs = outs[0], outs[1], outs[2], outs[3:]
    low = lax.ppermute(send, "gx", up)
    high = lax.ppermute(send, "gx", down)
    now, prev, keep, give = steps_two(where, place4, which, count, traces[0], send, low, high, fwd[ROUND:], iv, ib, *coefs)
    pair = keep + lax.ppermute(give, "shot", other_core)
    parts = jnp.sum(lax.all_to_all(pair, "shot", 0, 0, axis_index_groups=same_core), axis=0)
    scale = 1.0 / (SHOTS * STEPS) ** 0.5
    grad_vel = 2.0 * parts[:2] / velocity * scale
    grad_buoy = courant * velocity * velocity * (lap_unit * parts[2:]) * scale
    return grad_vel, grad_buoy, now[None], prev[None]


def solution(mesh):
    return jax.shard_map(
        shards,
        mesh=mesh,
        in_specs=(
            P("shot", "gx", "gy"),
            P("shot", "gx", "gy"),
            P("shot", None, None, "gx", "gy"),
            P("shot", None, "gx", "gy"),
            P("shot", None, "gx", "gy"),
            P("shot", None),
            P("shot", None, None),
        ),
        out_specs=(
            P("shot", "gx", "gy"),
            P("shot", "gx", "gy"),
            P("shot", None, "gx", "gy"),
            P("shot", None, "gx", "gy"),
        ),
        check_vma=False,
    )
```

```python
import functools

import jax
import jax.numpy as jnp
import numpy as np
from jax import lax
from jax.experimental import pallas as pl
from jax.experimental.pallas import tpu as pltpu
from jax.sharding import PartitionSpec as P

NZ, BX, BY = 16, 16, 128
FULL_X, FULL_Y = 256, 512
STEPS, SHOTS, RECV = 8, 8, 256
ROUND = 4
HY = 32
EXT = 3 * BX
PAD = 8
ROWS = EXT + 2 * PAD
LAYERS = NZ + 8
FAR = BY - HY
IMG = BX + 8

second_coef = (-205.0 / 72.0, 8.0 / 5.0, -1.0 / 5.0, 8.0 / 315.0, -1.0 / 560.0)
first_coef = (4.0 / 5.0, -1.0 / 5.0, 4.0 / 105.0, -1.0 / 280.0)
courant = 0.15
lap_unit = second_coef[4]
slope_unit = first_coef[3]
lap_ratio = (3.0 * second_coef[0] / lap_unit,) + tuple(c / lap_unit for c in second_coef[1:4])
slope_ratio = tuple(c / slope_unit for c in first_coef[:3])

VM = pl.BlockSpec(memory_space=pltpu.VMEM)
SM = pl.BlockSpec(memory_space=pltpu.SMEM)


def side_planes(groups):
    return NZ // groups + 8


def lane_of(rows):
    return lax.broadcasted_iota(jnp.int32, (rows, BY), 1)


def roll(x, shift):
    shift %= BY
    return pltpu.roll(x, shift, 1) if shift else x


def find_kernel(where_ref, recv_ref, place_ref, place4_ref, which_ref, count_ref):
    base_x = where_ref[0] - BX
    base_y = where_ref[1]

    def body(j, count):
        cell = recv_ref[j]
        z = lax.shift_right_logical(cell, 17)
        x = (lax.shift_right_logical(cell, 9) & (FULL_X - 1)) - base_x
        y = (cell & (FULL_Y - 1)) - base_y
        inside = (x >= 0) & (x < EXT) & (y >= -HY) & (y < BY + HY)
        main = (y >= 0) & (y < BY)
        right = y >= BY
        row = (x & 63) + PAD
        plane = jnp.where(main, z + 4, LAYERS + 4 + (z & 7))
        lane = jnp.where(main, y, lax.shift_right_logical(z, 3) * 64 + jnp.where(right, y - BY, y + 64))
        place_ref[count] = (plane * 64 + row) * 256 + (lane & 255)
        near = (y >= -16) & (y < BY + 16)
        plane = jnp.where(main, z + 4, LAYERS + 4 + (z & 3))
        lane = jnp.where(main, y, lax.shift_right_logical(z, 2) * 32 + jnp.where(right, y - BY, y + 32))
        lane = jnp.where(near, lane, 255)
        place4_ref[count] = (plane * 64 + row) * 256 + (lane & 255)
        which_ref[count] = j
        return count + inside.astype(jnp.int32)

    count = lax.fori_loop(0, RECV, body, jnp.int32(0), unroll=4)
    count_ref[0] = count
    for u in range(3):
        place_ref[count + u] = (4 * 64 + PAD) * 256 + 255
        place4_ref[count + u] = (4 * 64 + PAD) * 256 + 255
        which_ref[count + u] = 0


def pack_kernel(where_ref, fields_ref, model_ref, first_ref, second_ref):
    even = where_ref[2] == 0
    lane = lane_of(BX)
    out = 0
    for ref in (fields_ref, model_ref):
        for base in range(0, ref.shape[0], NZ):
            for q in range(4):
                right = left = None
                for i in range(4):
                    plane = ref[base + q + 4 * i]
                    j = i ^ 1
                    a, b = roll(plane, HY * j - FAR), roll(plane, HY * i)
                    right = a if right is None else jnp.where((lane >= HY * j) & (lane < HY * (j + 1)), a, right)
                    left = b if left is None else jnp.where((lane >= HY * i) & (lane < HY * (i + 1)), b, left)
                first_ref[out] = jnp.where(even, right, left)
                second_ref[out] = jnp.where(even, left, right)
                out += 1


def side_pair(first, second, even, lane):
    right = jnp.where(even, first, second)
    left = jnp.where(even, second, first)
    is_right = (lane & 63) < HY
    return (
        jnp.where(is_right, right, left),
        jnp.where(is_right, roll(right, -HY), roll(left, HY)),
    )


def four_from_two(near, far, lane):
    inner = (lane & 31) < 16
    own = (lane & 63) < 32
    return jnp.where(
        inner, jnp.where(own, near, roll(far, 32)), jnp.where(own, roll(near, -32), far)
    )


def repeat_sides(ref, groups):
    per = NZ // groups
    w = BY // groups
    rows = pl.ds(PAD, EXT)
    lane = lane_of(EXT)
    at = LAYERS + 4
    for i in range(4):
        after = roll(ref[at + i, rows, :], -w)
        ref[at + per + i, rows, :] = jnp.where(lane < BY - w, after, 0.0)
        before = roll(ref[at + per - 4 + i, rows, :], w)
        ref[at - 4 + i, rows, :] = jnp.where(lane >= w, before, 0.0)


def clear_ends(ref):
    for z in (0, 1, 2, 3, NZ + 4, NZ + 5, NZ + 6, NZ + 7):
        ref[z] = jnp.zeros(ref.shape[1:], jnp.float32)


PARTS = 3


def side_columns(groups):
    w = BY // groups
    lane = np.arange(BY)
    t = lane % w
    return lane // w, np.where(t < w // 2, BY + t, t - w)


def shift_weights(group_to, y_to, group_from, y_from):
    lap_k = np.array((0, 8064, -1008, 128, -9) + (0,) * 4, np.float32)
    slope_k = np.array((0, 672, -168, 32, -3) + (0,) * 4, np.float32)
    away = y_from[:, None] - y_to[None, :]
    k = np.where((group_from[:, None] == group_to[None, :]) & (abs(away) < 5), abs(away), 0)
    return np.concatenate([lap_k[k], slope_k[k] * np.sign(away)], axis=1)


def layer_weights(groups):
    side_group, side_y = side_columns(groups)
    y = np.arange(BY)
    both = []
    for g in range(groups):
        own = np.full(BY, g)
        both.append(np.concatenate([shift_weights(own, y, own, y), shift_weights(own, y, side_group, side_y)], axis=0))
    return jnp.asarray(np.stack(both), jnp.bfloat16)


def side_weights(groups):
    side_group, side_y = side_columns(groups)
    y = np.arange(BY)
    rows = [shift_weights(side_group, side_y, side_group, side_y)]
    rows += [shift_weights(side_group, side_y, np.full(BY, g), y) for g in range(groups)]
    return jnp.asarray(np.concatenate(rows, axis=0), jnp.bfloat16)


def shift_along_y(ref, groups, start, n, work, sides=True, lap_too=True):
    cut_layers, cut_sides, layer_w, side_w, y_lap, y_slope = work
    per = NZ // groups
    rows = pl.ds(PAD + start, n)

    def cut(at, to, z):
        x = ref[at, rows, :]
        for part in range(PARTS):
            piece = x.astype(jnp.bfloat16)
            to[part, z, pl.ds(0, n), :] = piece
            x = x - piece.astype(jnp.float32)

    def cut_group(p, _):
        for g in range(groups):
            cut(4 + p + g * per, cut_layers, p + g * per)
        cut(LAYERS + 4 + p, cut_sides, p)
        return 0

    lax.fori_loop(0, per, cut_group, 0, unroll=True)
    if sides:
        repeat_sides(ref, groups)

    def product(pieces, weights, first):
        weights = weights if lap_too else weights[:, BY:]
        stacked = jnp.concatenate([weights] * PARTS, axis=0)
        joined = jnp.concatenate(pieces, axis=1)
        half = per * n // 2 if first == NZ else per * n
        found = [jnp.dot(joined[i : i + half], stacked, preferred_element_type=jnp.float32) for i in range(0, per * n, half)]
        found = jnp.concatenate(found, axis=0) if len(found) > 1 else found[0]
        if lap_too:
            y_lap[first : first + per, pl.ds(start, n), :] = found[:, :BY].reshape(per, n, BY)
        y_slope[first : first + per, pl.ds(start, n), :] = found[:, -BY:].reshape(per, n, BY)

    def layer_piece(part, g):
        return cut_layers[part, g * per : (g + 1) * per, pl.ds(0, n), :].reshape(per * n, BY)

    def side_piece(part):
        return cut_sides[part, :, pl.ds(0, n), :].reshape(per * n, BY)

    for g in range(groups):
        pieces = [x for part in range(PARTS) for x in (layer_piece(part, g), side_piece(part))]
        product(pieces, layer_w[g], g * per)
    if sides:
        pieces = []
        for part in range(PARTS):
            pieces += [side_piece(part)] + [layer_piece(part, g) for g in range(groups)]
        product(pieces, side_w[...], NZ)


def along_zx(ref, at, row, n, lap_too=True):
    lap = dz = dx = None
    for k in (4, 3, 2, 1):
        zp = ref[at + k, pl.ds(row, n), :]
        zm = ref[at - k, pl.ds(row, n), :]
        xp = ref[at, pl.ds(row + k, n), :]
        xm = ref[at, pl.ds(row - k, n), :]
        if lap_too:
            both = (zp + zm) + (xp + xm)
            lap = both if k == 4 else lap + lap_ratio[k] * both
        c = slope_ratio[k - 1] if k < 4 else None
        dz = zp - zm if k == 4 else dz + c * (zp - zm)
        dx = xp - xm if k == 4 else dx + c * (xp - xm)
    return lap, dz, dx


def group_places(p, groups, sides=True):
    per = NZ // groups
    places = [(0, p + g * per, 4 + p + g * per, p + g * per) for g in range(groups)]
    return places + [(1, p, LAYERS + 4 + p, NZ + p)] * sides


PLANS = ((4, 12, 20, 28, 36), (8, 16, 24, 32), (12, 20, 28), (16, 24))
WINDOWS = ((0, 48), (8, 32), (8, 32), (16, 16))


def run_steps(first_step, groups, cur, old, coefs, fwd_ref, image, place_ref, which_ref, count_ref, trace_ref, work, last):
    lane1 = lane_of(1)
    y_lap, y_slope = work[-2:]
    for j, plan in enumerate(PLANS):

        def add(i, _, cur=cur, step=first_step + j):
            for u in range(4):
                place = place_ref[4 * i + u]
                value = trace_ref[step, which_ref[4 * i + u]]
                row = lax.shift_right_logical(place, 8) & 63
                spot = (lax.shift_right_logical(place, 14), pl.ds(row, 1), slice(None))
                cur[spot] = cur[spot] + jnp.where(lane1 == (place & 255), value, 0.0)
            return 0

        lax.fori_loop(0, lax.shift_right_logical(count_ref[0] + 3, 2), add, 0)
        sides = not (last and j == ROUND - 1)
        shift_along_y(cur, groups, *WINDOWS[j], work, sides)

        def layers(p, _, cur=cur, old=old, plan=plan, j=j, sides=sides):
            for lo in plan:
                rows = pl.ds(lo, 8)
                for kind, z, at, y in group_places(p, groups, sides):
                    lap, dz, dx = along_zx(cur, at, PAD + lo, 8)
                    spot = (at, pl.ds(PAD + lo, 8), slice(None))
                    here = cur[spot]
                    lap = (lap + (-1.0 / 9.0) * y_lap[y, rows, :]) + lap_ratio[0] * here
                    found = lap, dz, dx, y_slope[y, rows, :]
                    terms = [coefs[c][kind][z, rows, :] * found[c] for c in range(4)]
                    change = (terms[0] + terms[1]) + (terms[2] + terms[3])
                    old[spot] = ((here + here) - old[spot]) + change
                    if kind == 0 and BX - 8 < lo < 2 * BX:
                        seen = pl.ds(lo - (BX - 4), 8)
                        snapshot = fwd_ref[j, z, seen, :]
                        for total, term in zip(image, (snapshot * change, snapshot * lap)):
                            total[z, seen, :] = total[z, seen, :] + term if j else term
            return 0

        lax.fori_loop(0, NZ // groups, layers, 0)
        cur, old = old, cur
    return cur, old


def widen(fwd_ref, wide_ref):
    for step in range(ROUND):

        def body(z, _, step=step):
            wide_ref[step, z, pl.ds(4, BX), :] = fwd_ref[step, z].astype(jnp.float32)
            return 0

        lax.fori_loop(0, NZ, body, 0, unroll=4)


def first_kernel(
    where_ref, place_ref, which_ref, count_ref, trace_ref,
    centre_ref, low_ref, high_ref, centre_fields, low_fields, high_fields, other_ref, fwd_ref, layer_w, side_w,
    send_ref, iv_ref, ib_ref, m0, m1, m2, m3, f0, f1, f2, f3,
    cur, old, buoy, speed, speed_side, t0, t1, t2, t3, wide, cut_layers, cut_sides, y_lap, y_slope,
):
    work = cut_layers, cut_sides, layer_w, side_w, y_lap, y_slope
    even = where_ref[2] == 0
    core = where_ref[3]
    lane = lane_of(BX)
    for ref in (cur, old, buoy):
        clear_ends(ref)
    widen(fwd_ref, wide)
    at = LAYERS + 4
    blocks = ((low_ref, low_fields), (centre_ref, centre_fields), (high_ref, high_fields))
    for block, (ref, fields) in enumerate(blocks):
        rows = pl.ds(PAD + block * BX, BX)
        bare = pl.ds(block * BX, BX)
        for f, field in enumerate((cur, old)):
            for z in range(NZ):
                field[4 + z, rows, :] = fields[NZ * f + z]
            for q in range(4):
                near, far = side_pair(ref[16 + 4 * f + q], ref[28 + 4 * f + q], even, lane)
                field[at + q, rows, :] = near
                field[at + q + 4, rows, :] = far
        for half in (0, 1):
            turn = core if half == 0 else 1 - core
            spot = (1, 0, 2)[block]
            for t in range(4):
                z = 2 * turn + t % 2
                if half == 0:
                    planes = [ref[4 * i + t] for i in range(4)]
                    packs = ref[24 + t], ref[36 + t]
                else:
                    planes = [other_ref[24 * spot + 4 * i + t] for i in range(4)]
                    packs = other_ref[24 * spot + 16 + t], other_ref[24 * spot + 20 + t]
                pair = side_pair(*packs, even, lane)
                if t < 2:
                    for i in range(4):
                        speed[z + 4 * i, bare, :] = courant * planes[i] * planes[i]
                    for i in range(2):
                        speed_side[z + 4 * i, bare, :] = courant * pair[i] * pair[i]
                else:
                    for i in range(4):
                        buoy[4 + z + 4 * i, rows, :] = planes[i]
                    for i in range(2):
                        buoy[at + z + 4 * i, rows, :] = pair[i]
    coefs = ((m0, t0), (m1, t1), (m2, t2), (m3, t3))

    shift_along_y(buoy, 2, 0, EXT, work, lap_too=False)

    def slopes(p, _):
        for lo in PLANS[0]:
            rows = pl.ds(lo, 8)
            for kind, z, at, y in group_places(p, 2):
                _lap, dz, dx = along_zx(buoy, at, PAD + lo, 8, lap_too=False)
                pace = (speed, speed_side)[kind][z, rows, :]
                coefs[0][kind][z, rows, :] = (lap_unit * pace) * buoy[at, pl.ds(PAD + lo, 8), :]
                steep = (slope_unit * slope_unit) * pace
                coefs[1][kind][z, rows, :] = steep * dz
                coefs[2][kind][z, rows, :] = steep * dx
                coefs[3][kind][z, rows, :] = ((1.0 / 840.0 / 840.0) * pace) * y_slope[y, rows, :]
        return 0

    lax.fori_loop(0, NZ // 2, slopes, 0)
    lane8 = lane_of(8)
    for wide_side, side in ((t0, f0), (t1, f1), (t2, f2), (t3, f3)):
        for p in range(4):
            for lo in PLANS[0]:
                rows = pl.ds(lo, 8)
                side[p, rows, :] = four_from_two(wide_side[p, rows, :], wide_side[p + 4, rows, :], lane8)
    now, prev = run_steps(
        0, 2, cur, old, coefs, wide, (iv_ref, ib_ref), place_ref, which_ref, count_ref, trace_ref, work, False
    )
    rows = pl.ds(PAD + BX, BX)
    for f, field in enumerate((now, prev)):
        for z in range(NZ):
            send_ref[NZ * f + z] = field[4 + z, rows, :]
        for p in range(4):
            send_ref[2 * NZ + 4 * f + p] = four_from_two(field[at + p, rows, :], field[at + p + 4, rows, :], lane)


def second_kernel(
    where_ref, place_ref, which_ref, count_ref, trace_ref,
    centre_ref, low_ref, high_ref, fwd_ref, iv_ref, ib_ref, m0, m1, m2, m3, f0, f1, f2, f3, layer_w, side_w,
    now_ref, prev_ref, keep_ref, give_ref,
    cur, old, iv, ib, wide, cut_layers, cut_sides, y_lap, y_slope,
):
    work = cut_layers, cut_sides, layer_w, side_w, y_lap, y_slope
    for ref in (cur, old):
        clear_ends(ref)
    widen(fwd_ref, wide)
    at = LAYERS + 4
    for block, ref in enumerate((low_ref, centre_ref, high_ref)):
        rows = pl.ds(PAD + block * BX, BX)
        for f, field in enumerate((cur, old)):
            for z in range(NZ):
                field[4 + z, rows, :] = ref[NZ * f + z]
            for p in range(4):
                field[at + p, rows, :] = ref[2 * NZ + 4 * f + p]
    now, prev = run_steps(
        ROUND, 4, cur, old, ((m0, f0), (m1, f1), (m2, f2), (m3, f3)), wide, (iv, ib),
        place_ref, which_ref, count_ref, trace_ref, work, True,
    )
    rows = pl.ds(PAD + BX, BX)
    wanted = pl.ds(4, BX)
    core = where_ref[3]
    for z in range(NZ):
        now_ref[z] = now[4 + z, rows, :]
        prev_ref[z] = prev[4 + z, rows, :]
    for i in range(4):
        for ref, turn in ((keep_ref, core), (give_ref, 1 - core)):
            for v in (0, 1):
                z = 4 * i + 2 * turn + v
                ref[i, v] = iv[z, wanted, :] + iv_ref[z, wanted, :]
                ref[i, 2 + v] = ib[z, wanted, :] + ib_ref[z, wanted, :]


def shape(*dims, dtype=jnp.float32):
    return jax.ShapeDtypeStruct(dims, dtype)


def room(mib):
    return pltpu.CompilerParams(vmem_limit_bytes=mib * 1024 * 1024)


PARAMS = room(32)


def buffer(*dims):
    return pltpu.VMEM(dims, jnp.float32)


def work_buffers(groups):
    planes = NZ + NZ // groups
    return [
        pltpu.VMEM((PARTS, NZ, EXT, BY), jnp.bfloat16),
        pltpu.VMEM((PARTS, NZ // groups, EXT, BY), jnp.bfloat16),
        buffer(planes, EXT, BY),
        buffer(planes, EXT, BY),
    ]


def steps_one(*operands):
    ext, side_ext = shape(NZ, EXT, BY), shape(NZ // 4, EXT, BY)
    image = shape(NZ, IMG, BY)
    block = LAYERS + side_planes(2)
    return pl.pallas_call(
        first_kernel,
        out_shape=(shape(40, BX, BY), image, image) + (ext,) * 4 + (side_ext,) * 4,
        in_specs=[SM] * 5 + [VM] * 10,
        out_specs=(VM,) * 11,
        scratch_shapes=[buffer(block, ROWS, BY)] * 3
        + [buffer(NZ, EXT, BY)]
        + [buffer(NZ // 2, EXT, BY)] * 5
        + [buffer(ROUND, NZ, IMG, BY)]
        + work_buffers(2),
        compiler_params=PARAMS,
        name="first_steps",
    )(*operands, layer_weights(2), side_weights(2))


def steps_two(*operands):
    block = LAYERS + side_planes(4)
    return pl.pallas_call(
        second_kernel,
        out_shape=(shape(NZ, BX, BY),) * 2 + (shape(4, 4, BX, BY),) * 2,
        in_specs=[SM] * 5 + [VM] * 16,
        out_specs=(VM,) * 4,
        scratch_shapes=[buffer(block, ROWS, BY)] * 2 + [buffer(NZ, IMG, BY)] * 2
        + [buffer(ROUND, NZ, IMG, BY)]
        + work_buffers(4),
        compiler_params=PARAMS,
        name="second_steps",
    )(*operands, layer_weights(4), side_weights(4))


def swap(x, axis, pairs):
    return lax.ppermute(x, axis, [(a, b) for a, b in pairs] + [(b, a) for a, b in pairs])


def shards(velocity, buoyancy, fwd_field, adjoint_now, adjoint_prev, recv_cell, traces):
    now, prev, fwd = adjoint_now[0], adjoint_prev[0], fwd_field[0]
    gx, gy, shot = lax.axis_index("gx"), lax.axis_index("gy"), lax.axis_index("shot")
    where = jnp.stack([gx * BX, gy * BY, gy % 2, shot % 2]).astype(jnp.int32)
    same_core = [list(range(core, SHOTS, 2)) for core in (0, 1)]
    other_core = [(i, i ^ 1) for i in range(SHOTS)]
    count_y, count_x = lax.axis_size("gy"), lax.axis_size("gx")

    listed = shape(RECV + 8, dtype=jnp.int32)
    place, place4, which, count = pl.pallas_call(
        find_kernel,
        out_shape=(listed, listed, listed, shape(1, dtype=jnp.int32)),
        in_specs=[SM, SM],
        out_specs=(SM,) * 4,
        compiler_params=room(4),
        cost_estimate=pl.CostEstimate(flops=8000, bytes_accessed=4000, transcendentals=0),
        name="find_receivers",
    )(where, recv_cell[0])

    up = [(i, i + 1) for i in range(count_x - 1)]
    down = [(b, a) for a, b in up]
    fields = jnp.concatenate([now, prev], axis=0)
    low_fields = lax.ppermute(fields, "gx", up)
    high_fields = lax.ppermute(fields, "gx", down)

    own = jnp.concatenate([jnp.broadcast_to(part, (4,) + part.shape) for part in (velocity, buoyancy)], axis=1)
    half = lax.all_to_all(own, "shot", 0, 0, axis_index_groups=same_core).reshape(16, BX, BY)

    first, second = pl.pallas_call(
        pack_kernel,
        out_shape=(shape(12, BX, BY), shape(12, BX, BY)),
        in_specs=[SM, VM, VM],
        out_specs=(VM, VM),
        compiler_params=room(8),
        name="pack_sides",
    )(where, fields, half)
    first = swap(first, "gy", [(i, i + 1) for i in range(0, count_y, 2)])
    second = swap(second, "gy", [(i, i + 1) for i in range(1, count_y - 1, 2)])

    centre = jnp.concatenate([half, first, second], axis=0)
    centre, low_fields, high_fields, place, place4, which, count = lax.optimization_barrier(
        (centre, low_fields, high_fields, place, place4, which, count)
    )
    low = lax.ppermute(centre, "gx", up)
    high = lax.ppermute(centre, "gx", down)

    model = jnp.concatenate(
        [part for block in (centre, low, high) for part in (block[0:16], block[24:28], block[36:40])], axis=0
    )
    other = lax.ppermute(model, "shot", other_core)

    outs = steps_one(
        where, place, which, count, traces[0], centre, low, high, fields, low_fields, high_fields, other, fwd[:ROUND]
    )
    send, iv, ib, coefs = outs[0], outs[1], outs[2], outs[3:]
    low = lax.ppermute(send, "gx", up)
    high = lax.ppermute(send, "gx", down)
    now, prev, keep, give = steps_two(where, place4, which, count, traces[0], send, low, high, fwd[ROUND:], iv, ib, *coefs)
    pair = keep + lax.ppermute(give, "shot", other_core)
    parts = jnp.sum(lax.all_to_all(pair, "shot", 0, 0, axis_index_groups=same_core), axis=0)
    scale = 1.0 / (SHOTS * STEPS) ** 0.5
    grad_vel = 2.0 * parts[:2] / velocity * scale
    grad_buoy = courant * velocity * velocity * (lap_unit * parts[2:]) * scale
    return grad_vel, grad_buoy, now[None], prev[None]


def solution(mesh):
    return jax.shard_map(
        shards,
        mesh=mesh,
        in_specs=(
            P("shot", "gx", "gy"),
            P("shot", "gx", "gy"),
            P("shot", None, None, "gx", "gy"),
            P("shot", None, "gx", "gy"),
            P("shot", None, "gx", "gy"),
            P("shot", None),
            P("shot", None, None),
        ),
        out_specs=(
            P("shot", "gx", "gy"),
            P("shot", "gx", "gy"),
            P("shot", None, "gx", "gy"),
            P("shot", None, "gx", "gy"),
        ),
        check_vma=False,
    )
```

```python
import functools

import jax
import jax.numpy as jnp
import numpy as np
from jax import lax
from jax.experimental import pallas as pl
from jax.experimental.pallas import tpu as pltpu
from jax.sharding import PartitionSpec as P

NZ, BX, BY = 16, 16, 128
FULL_X, FULL_Y = 256, 512
STEPS, SHOTS, RECV = 8, 8, 256
ROUND = 4
HY = 32
EXT = 3 * BX
PAD = 8
ROWS = EXT + 2 * PAD
LAYERS = NZ + 8
FAR = BY - HY
IMG = BX + 8

second_coef = (-205.0 / 72.0, 8.0 / 5.0, -1.0 / 5.0, 8.0 / 315.0, -1.0 / 560.0)
first_coef = (4.0 / 5.0, -1.0 / 5.0, 4.0 / 105.0, -1.0 / 280.0)
courant = 0.15
lap_unit = second_coef[4]
slope_unit = first_coef[3]
lap_ratio = (3.0 * second_coef[0] / lap_unit,) + tuple(c / lap_unit for c in second_coef[1:4])
slope_ratio = tuple(c / slope_unit for c in first_coef[:3])

VM = pl.BlockSpec(memory_space=pltpu.VMEM)
SM = pl.BlockSpec(memory_space=pltpu.SMEM)


def side_planes(groups):
    return NZ // groups + 8


def lane_of(rows):
    return lax.broadcasted_iota(jnp.int32, (rows, BY), 1)


def roll(x, shift):
    shift %= BY
    return pltpu.roll(x, shift, 1) if shift else x


def find_kernel(where_ref, recv_ref, place_ref, place4_ref, which_ref, count_ref):
    base_x = where_ref[0] - BX
    base_y = where_ref[1]

    def body(j, count):
        cell = recv_ref[j]
        z = lax.shift_right_logical(cell, 17)
        x = (lax.shift_right_logical(cell, 9) & (FULL_X - 1)) - base_x
        y = (cell & (FULL_Y - 1)) - base_y
        inside = (x >= 0) & (x < EXT) & (y >= -HY) & (y < BY + HY)
        main = (y >= 0) & (y < BY)
        right = y >= BY
        row = (x & 63) + PAD
        plane = jnp.where(main, z + 4, LAYERS + 4 + (z & 7))
        lane = jnp.where(main, y, lax.shift_right_logical(z, 3) * 64 + jnp.where(right, y - BY, y + 64))
        place_ref[count] = (plane * 64 + row) * 256 + (lane & 255)
        near = (y >= -16) & (y < BY + 16)
        plane = jnp.where(main, z + 4, LAYERS + 4 + (z & 3))
        lane = jnp.where(main, y, lax.shift_right_logical(z, 2) * 32 + jnp.where(right, y - BY, y + 32))
        lane = jnp.where(near, lane, 255)
        place4_ref[count] = (plane * 64 + row) * 256 + (lane & 255)
        which_ref[count] = j
        return count + inside.astype(jnp.int32)

    count = lax.fori_loop(0, RECV, body, jnp.int32(0), unroll=4)
    count_ref[0] = count
    for u in range(3):
        place_ref[count + u] = (4 * 64 + PAD) * 256 + 255
        place4_ref[count + u] = (4 * 64 + PAD) * 256 + 255
        which_ref[count + u] = 0


def pack_kernel(where_ref, fields_ref, model_ref, first_ref, second_ref):
    even = where_ref[2] == 0
    lane = lane_of(BX)
    out = 0
    for ref in (fields_ref, model_ref):
        for base in range(0, ref.shape[0], NZ):
            for q in range(4):
                right = left = None
                for i in range(4):
                    plane = ref[base + q + 4 * i]
                    j = i ^ 1
                    a, b = roll(plane, HY * j - FAR), roll(plane, HY * i)
                    right = a if right is None else jnp.where((lane >= HY * j) & (lane < HY * (j + 1)), a, right)
                    left = b if left is None else jnp.where((lane >= HY * i) & (lane < HY * (i + 1)), b, left)
                first_ref[out] = jnp.where(even, right, left)
                second_ref[out] = jnp.where(even, left, right)
                out += 1


def side_pair(first, second, even, lane):
    right = jnp.where(even, first, second)
    left = jnp.where(even, second, first)
    is_right = (lane & 63) < HY
    return (
        jnp.where(is_right, right, left),
        jnp.where(is_right, roll(right, -HY), roll(left, HY)),
    )


def four_from_two(near, far, lane):
    inner = (lane & 31) < 16
    own = (lane & 63) < 32
    return jnp.where(
        inner, jnp.where(own, near, roll(far, 32)), jnp.where(own, roll(near, -32), far)
    )


def repeat_sides(ref, groups):
    per = NZ // groups
    w = BY // groups
    rows = pl.ds(PAD, EXT)
    lane = lane_of(EXT)
    at = LAYERS + 4
    for i in range(4):
        after = roll(ref[at + i, rows, :], -w)
        ref[at + per + i, rows, :] = jnp.where(lane < BY - w, after, 0.0)
        before = roll(ref[at + per - 4 + i, rows, :], w)
        ref[at - 4 + i, rows, :] = jnp.where(lane >= w, before, 0.0)


def clear_ends(ref):
    for z in (0, 1, 2, 3, NZ + 4, NZ + 5, NZ + 6, NZ + 7):
        ref[z] = jnp.zeros(ref.shape[1:], jnp.float32)


PARTS = 3


def side_columns(groups):
    w = BY // groups
    lane = np.arange(BY)
    t = lane % w
    return lane // w, np.where(t < w // 2, BY + t, t - w)


def shift_weights(group_to, y_to, group_from, y_from):
    lap_k = np.array((0, 8064, -1008, 128, -9) + (0,) * 4, np.float32)
    slope_k = np.array((0, 672, -168, 32, -3) + (0,) * 4, np.float32)
    away = y_from[:, None] - y_to[None, :]
    k = np.where((group_from[:, None] == group_to[None, :]) & (abs(away) < 5), abs(away), 0)
    return np.concatenate([lap_k[k], slope_k[k] * np.sign(away)], axis=1)


def layer_weights(groups):
    side_group, side_y = side_columns(groups)
    y = np.arange(BY)
    both = []
    for g in range(groups):
        own = np.full(BY, g)
        both.append(np.concatenate([shift_weights(own, y, own, y), shift_weights(own, y, side_group, side_y)], axis=0))
    return jnp.asarray(np.stack(both), jnp.bfloat16)


def side_weights(groups):
    side_group, side_y = side_columns(groups)
    y = np.arange(BY)
    rows = [shift_weights(side_group, side_y, side_group, side_y)]
    rows += [shift_weights(side_group, side_y, np.full(BY, g), y) for g in range(groups)]
    return jnp.asarray(np.concatenate(rows, axis=0), jnp.bfloat16)


def shift_along_y(ref, groups, start, n, work, sides=True, lap_too=True):
    cut_layers, cut_sides, layer_w, side_w, y_lap, y_slope = work
    per = NZ // groups
    rows = pl.ds(PAD + start, n)

    def cut(at, to, z):
        x = ref[at, rows, :]
        for part in range(PARTS):
            piece = x.astype(jnp.bfloat16)
            to[part, z, pl.ds(0, n), :] = piece
            x = x - piece.astype(jnp.float32)

    def cut_group(p, _):
        for g in range(groups):
            cut(4 + p + g * per, cut_layers, p + g * per)
        cut(LAYERS + 4 + p, cut_sides, p)
        return 0

    lax.fori_loop(0, per, cut_group, 0, unroll=True)
    if sides:
        repeat_sides(ref, groups)

    def product(pieces, weights, first):
        weights = weights if lap_too else weights[:, BY:]
        stacked = jnp.concatenate([weights] * PARTS, axis=0)
        joined = jnp.concatenate(pieces, axis=1)
        half = per * n // 2 if first == NZ else per * n
        found = [jnp.dot(joined[i : i + half], stacked, preferred_element_type=jnp.float32) for i in range(0, per * n, half)]
        found = jnp.concatenate(found, axis=0) if len(found) > 1 else found[0]
        if lap_too:
            y_lap[first : first + per, pl.ds(start, n), :] = found[:, :BY].reshape(per, n, BY)
        y_slope[first : first + per, pl.ds(start, n), :] = found[:, -BY:].reshape(per, n, BY)

    def layer_piece(part, g):
        return cut_layers[part, g * per : (g + 1) * per, pl.ds(0, n), :].reshape(per * n, BY)

    def side_piece(part):
        return cut_sides[part, :, pl.ds(0, n), :].reshape(per * n, BY)

    for g in range(groups):
        pieces = [x for part in range(PARTS) for x in (layer_piece(part, g), side_piece(part))]
        product(pieces, layer_w[g], g * per)
    if sides:
        pieces = []
        for part in range(PARTS):
            pieces += [side_piece(part)] + [layer_piece(part, g) for g in range(groups)]
        product(pieces, side_w[...], NZ)


def along_zx(ref, at, row, n, lap_too=True):
    lap = dz = dx = None
    for k in (4, 3, 2, 1):
        zp = ref[at + k, pl.ds(row, n), :]
        zm = ref[at - k, pl.ds(row, n), :]
        xp = ref[at, pl.ds(row + k, n), :]
        xm = ref[at, pl.ds(row - k, n), :]
        if lap_too:
            both = (zp + zm) + (xp + xm)
            lap = both if k == 4 else lap + lap_ratio[k] * both
        c = slope_ratio[k - 1] if k < 4 else None
        dz = zp - zm if k == 4 else dz + c * (zp - zm)
        dx = xp - xm if k == 4 else dx + c * (xp - xm)
    return lap, dz, dx


def group_places(p, groups, sides=True):
    per = NZ // groups
    places = [(0, p + g * per, 4 + p + g * per, p + g * per) for g in range(groups)]
    return places + [(1, p, LAYERS + 4 + p, NZ + p)] * sides


PLANS = ((4, 12, 20, 28, 36), (8, 16, 24, 32), (12, 20, 28), (16, 24))
WINDOWS = ((0, 48), (8, 32), (8, 32), (16, 16))


def run_steps(first_step, groups, cur, old, coefs, fwd_ref, image, place_ref, which_ref, count_ref, trace_ref, work, last):
    lane1 = lane_of(1)
    y_lap, y_slope = work[-2:]
    for j, plan in enumerate(PLANS):

        def add(i, _, cur=cur, step=first_step + j):
            for u in range(4):
                place = place_ref[4 * i + u]
                value = trace_ref[step, which_ref[4 * i + u]]
                row = lax.shift_right_logical(place, 8) & 63
                spot = (lax.shift_right_logical(place, 14), pl.ds(row, 1), slice(None))
                cur[spot] = cur[spot] + jnp.where(lane1 == (place & 255), value, 0.0)
            return 0

        lax.fori_loop(0, lax.shift_right_logical(count_ref[0] + 3, 2), add, 0)
        sides = not (last and j == ROUND - 1)
        shift_along_y(cur, groups, *WINDOWS[j], work, sides)

        def layers(p, _, cur=cur, old=old, plan=plan, j=j, sides=sides):
            for lo in plan:
                rows = pl.ds(lo, 8)
                for kind, z, at, y in group_places(p, groups, sides):
                    lap, dz, dx = along_zx(cur, at, PAD + lo, 8)
                    spot = (at, pl.ds(PAD + lo, 8), slice(None))
                    here = cur[spot]
                    lap = (lap + (-1.0 / 9.0) * y_lap[y, rows, :]) + lap_ratio[0] * here
                    found = lap, dz, dx, y_slope[y, rows, :]
                    terms = [coefs[c][kind][z, rows, :] * found[c] for c in range(4)]
                    change = (terms[0] + terms[1]) + (terms[2] + terms[3])
                    old[spot] = ((here + here) - old[spot]) + change
                    if kind == 0 and BX - 8 < lo < 2 * BX:
                        seen = pl.ds(lo - (BX - 4), 8)
                        snapshot = fwd_ref[j, z, seen, :]
                        for total, term in zip(image, (snapshot * change, snapshot * lap)):
                            total[z, seen, :] = total[z, seen, :] + term if j else term
            return 0

        lax.fori_loop(0, NZ // groups, layers, 0, unroll=4)
        cur, old = old, cur
    return cur, old


def widen(fwd_ref, wide_ref):
    for step in range(ROUND):

        def body(z, _, step=step):
            wide_ref[step, z, pl.ds(4, BX), :] = fwd_ref[step, z].astype(jnp.float32)
            return 0

        lax.fori_loop(0, NZ, body, 0, unroll=4)


def first_kernel(
    where_ref, place_ref, which_ref, count_ref, trace_ref,
    centre_ref, low_ref, high_ref, centre_fields, low_fields, high_fields, other_ref, fwd_ref, layer_w, side_w,
    send_ref, iv_ref, ib_ref, m0, m1, m2, m3, f0, f1, f2, f3,
    cur, old, buoy, speed, speed_side, t0, t1, t2, t3, wide, cut_layers, cut_sides, y_lap, y_slope,
):
    work = cut_layers, cut_sides, layer_w, side_w, y_lap, y_slope
    even = where_ref[2] == 0
    core = where_ref[3]
    lane = lane_of(BX)
    for ref in (cur, old, buoy):
        clear_ends(ref)
    widen(fwd_ref, wide)
    at = LAYERS + 4
    blocks = ((low_ref, low_fields), (centre_ref, centre_fields), (high_ref, high_fields))
    for block, (ref, fields) in enumerate(blocks):
        rows = pl.ds(PAD + block * BX, BX)
        bare = pl.ds(block * BX, BX)
        for f, field in enumerate((cur, old)):
            for z in range(NZ):
                field[4 + z, rows, :] = fields[NZ * f + z]
            for q in range(4):
                near, far = side_pair(ref[16 + 4 * f + q], ref[28 + 4 * f + q], even, lane)
                field[at + q, rows, :] = near
                field[at + q + 4, rows, :] = far
        for half in (0, 1):
            turn = core if half == 0 else 1 - core
            spot = (1, 0, 2)[block]
            for t in range(4):
                z = 2 * turn + t % 2
                if half == 0:
                    planes = [ref[4 * i + t] for i in range(4)]
                    packs = ref[24 + t], ref[36 + t]
                else:
                    planes = [other_ref[24 * spot + 4 * i + t] for i in range(4)]
                    packs = other_ref[24 * spot + 16 + t], other_ref[24 * spot + 20 + t]
                pair = side_pair(*packs, even, lane)
                if t < 2:
                    for i in range(4):
                        speed[z + 4 * i, bare, :] = courant * planes[i] * planes[i]
                    for i in range(2):
                        speed_side[z + 4 * i, bare, :] = courant * pair[i] * pair[i]
                else:
                    for i in range(4):
                        buoy[4 + z + 4 * i, rows, :] = planes[i]
                    for i in range(2):
                        buoy[at + z + 4 * i, rows, :] = pair[i]
    coefs = ((m0, t0), (m1, t1), (m2, t2), (m3, t3))

    shift_along_y(buoy, 2, 0, EXT, work, lap_too=False)

    def slopes(p, _):
        for lo in PLANS[0]:
            rows = pl.ds(lo, 8)
            for kind, z, at, y in group_places(p, 2):
                _lap, dz, dx = along_zx(buoy, at, PAD + lo, 8, lap_too=False)
                pace = (speed, speed_side)[kind][z, rows, :]
                coefs[0][kind][z, rows, :] = (lap_unit * pace) * buoy[at, pl.ds(PAD + lo, 8), :]
                steep = (slope_unit * slope_unit) * pace
                coefs[1][kind][z, rows, :] = steep * dz
                coefs[2][kind][z, rows, :] = steep * dx
                coefs[3][kind][z, rows, :] = ((1.0 / 840.0 / 840.0) * pace) * y_slope[y, rows, :]
        return 0

    lax.fori_loop(0, NZ // 2, slopes, 0, unroll=2)
    lane8 = lane_of(8)
    for wide_side, side in ((t0, f0), (t1, f1), (t2, f2), (t3, f3)):
        for p in range(4):
            for lo in PLANS[0]:
                rows = pl.ds(lo, 8)
                side[p, rows, :] = four_from_two(wide_side[p, rows, :], wide_side[p + 4, rows, :], lane8)
    now, prev = run_steps(
        0, 2, cur, old, coefs, wide, (iv_ref, ib_ref), place_ref, which_ref, count_ref, trace_ref, work, False
    )
    rows = pl.ds(PAD + BX, BX)
    for f, field in enumerate((now, prev)):
        for z in range(NZ):
            send_ref[NZ * f + z] = field[4 + z, rows, :]
        for p in range(4):
            send_ref[2 * NZ + 4 * f + p] = four_from_two(field[at + p, rows, :], field[at + p + 4, rows, :], lane)


def second_kernel(
    where_ref, place_ref, which_ref, count_ref, trace_ref,
    centre_ref, low_ref, high_ref, fwd_ref, iv_ref, ib_ref, m0, m1, m2, m3, f0, f1, f2, f3, layer_w, side_w,
    now_ref, prev_ref, keep_ref, give_ref,
    cur, old, iv, ib, wide, cut_layers, cut_sides, y_lap, y_slope,
):
    work = cut_layers, cut_sides, layer_w, side_w, y_lap, y_slope
    for ref in (cur, old):
        clear_ends(ref)
    widen(fwd_ref, wide)
    at = LAYERS + 4
    for block, ref in enumerate((low_ref, centre_ref, high_ref)):
        rows = pl.ds(PAD + block * BX, BX)
        for f, field in enumerate((cur, old)):
            for z in range(NZ):
                field[4 + z, rows, :] = ref[NZ * f + z]
            for p in range(4):
                field[at + p, rows, :] = ref[2 * NZ + 4 * f + p]
    now, prev = run_steps(
        ROUND, 4, cur, old, ((m0, f0), (m1, f1), (m2, f2), (m3, f3)), wide, (iv, ib),
        place_ref, which_ref, count_ref, trace_ref, work, True,
    )
    rows = pl.ds(PAD + BX, BX)
    wanted = pl.ds(4, BX)
    core = where_ref[3]
    for z in range(NZ):
        now_ref[z] = now[4 + z, rows, :]
        prev_ref[z] = prev[4 + z, rows, :]
    for i in range(4):
        for ref, turn in ((keep_ref, core), (give_ref, 1 - core)):
            for v in (0, 1):
                z = 4 * i + 2 * turn + v
                ref[i, v] = iv[z, wanted, :] + iv_ref[z, wanted, :]
                ref[i, 2 + v] = ib[z, wanted, :] + ib_ref[z, wanted, :]


def shape(*dims, dtype=jnp.float32):
    return jax.ShapeDtypeStruct(dims, dtype)


def room(mib):
    return pltpu.CompilerParams(vmem_limit_bytes=mib * 1024 * 1024)


PARAMS = room(32)


def buffer(*dims):
    return pltpu.VMEM(dims, jnp.float32)


def work_buffers(groups):
    planes = NZ + NZ // groups
    return [
        pltpu.VMEM((PARTS, NZ, EXT, BY), jnp.bfloat16),
        pltpu.VMEM((PARTS, NZ // groups, EXT, BY), jnp.bfloat16),
        buffer(planes, EXT, BY),
        buffer(planes, EXT, BY),
    ]


def steps_one(*operands):
    ext, side_ext = shape(NZ, EXT, BY), shape(NZ // 4, EXT, BY)
    image = shape(NZ, IMG, BY)
    block = LAYERS + side_planes(2)
    return pl.pallas_call(
        first_kernel,
        out_shape=(shape(40, BX, BY), image, image) + (ext,) * 4 + (side_ext,) * 4,
        in_specs=[SM] * 5 + [VM] * 10,
        out_specs=(VM,) * 11,
        scratch_shapes=[buffer(block, ROWS, BY)] * 3
        + [buffer(NZ, EXT, BY)]
        + [buffer(NZ // 2, EXT, BY)] * 5
        + [buffer(ROUND, NZ, IMG, BY)]
        + work_buffers(2),
        compiler_params=PARAMS,
        name="first_steps",
    )(*operands, layer_weights(2), side_weights(2))


def steps_two(*operands):
    block = LAYERS + side_planes(4)
    return pl.pallas_call(
        second_kernel,
        out_shape=(shape(NZ, BX, BY),) * 2 + (shape(4, 4, BX, BY),) * 2,
        in_specs=[SM] * 5 + [VM] * 16,
        out_specs=(VM,) * 4,
        scratch_shapes=[buffer(block, ROWS, BY)] * 2 + [buffer(NZ, IMG, BY)] * 2
        + [buffer(ROUND, NZ, IMG, BY)]
        + work_buffers(4),
        compiler_params=PARAMS,
        name="second_steps",
    )(*operands, layer_weights(4), side_weights(4))


def swap(x, axis, pairs):
    return lax.ppermute(x, axis, [(a, b) for a, b in pairs] + [(b, a) for a, b in pairs])


def shards(velocity, buoyancy, fwd_field, adjoint_now, adjoint_prev, recv_cell, traces):
    now, prev, fwd = adjoint_now[0], adjoint_prev[0], fwd_field[0]
    gx, gy, shot = lax.axis_index("gx"), lax.axis_index("gy"), lax.axis_index("shot")
    where = jnp.stack([gx * BX, gy * BY, gy % 2, shot % 2]).astype(jnp.int32)
    same_core = [list(range(core, SHOTS, 2)) for core in (0, 1)]
    other_core = [(i, i ^ 1) for i in range(SHOTS)]
    count_y, count_x = lax.axis_size("gy"), lax.axis_size("gx")

    listed = shape(RECV + 8, dtype=jnp.int32)
    place, place4, which, count = pl.pallas_call(
        find_kernel,
        out_shape=(listed, listed, listed, shape(1, dtype=jnp.int32)),
        in_specs=[SM, SM],
        out_specs=(SM,) * 4,
        compiler_params=room(4),
        cost_estimate=pl.CostEstimate(flops=8000, bytes_accessed=4000, transcendentals=0),
        name="find_receivers",
    )(where, recv_cell[0])

    up = [(i, i + 1) for i in range(count_x - 1)]
    down = [(b, a) for a, b in up]
    fields = jnp.concatenate([now, prev], axis=0)
    low_fields = lax.ppermute(fields, "gx", up)
    high_fields = lax.ppermute(fields, "gx", down)

    own = jnp.concatenate([jnp.broadcast_to(part, (4,) + part.shape) for part in (velocity, buoyancy)], axis=1)
    half = lax.all_to_all(own, "shot", 0, 0, axis_index_groups=same_core).reshape(16, BX, BY)

    first, second = pl.pallas_call(
        pack_kernel,
        out_shape=(shape(12, BX, BY), shape(12, BX, BY)),
        in_specs=[SM, VM, VM],
        out_specs=(VM, VM),
        compiler_params=room(8),
        name="pack_sides",
    )(where, fields, half)
    first = swap(first, "gy", [(i, i + 1) for i in range(0, count_y, 2)])
    second = swap(second, "gy", [(i, i + 1) for i in range(1, count_y - 1, 2)])

    centre = jnp.concatenate([half, first, second], axis=0)
    centre, low_fields, high_fields, place, place4, which, count = lax.optimization_barrier(
        (centre, low_fields, high_fields, place, place4, which, count)
    )
    low = lax.ppermute(centre, "gx", up)
    high = lax.ppermute(centre, "gx", down)

    model = jnp.concatenate(
        [part for block in (centre, low, high) for part in (block[0:16], block[24:28], block[36:40])], axis=0
    )
    other = lax.ppermute(model, "shot", other_core)

    outs = steps_one(
        where, place, which, count, traces[0], centre, low, high, fields, low_fields, high_fields, other, fwd[:ROUND]
    )
    send, iv, ib, coefs = outs[0], outs[1], outs[2], outs[3:]
    low = lax.ppermute(send, "gx", up)
    high = lax.ppermute(send, "gx", down)
    now, prev, keep, give = steps_two(where, place4, which, count, traces[0], send, low, high, fwd[ROUND:], iv, ib, *coefs)
    pair = keep + lax.ppermute(give, "shot", other_core)
    parts = jnp.sum(lax.all_to_all(pair, "shot", 0, 0, axis_index_groups=same_core), axis=0)
    scale = 1.0 / (SHOTS * STEPS) ** 0.5
    grad_vel = 2.0 * parts[:2] / velocity * scale
    grad_buoy = courant * velocity * velocity * (lap_unit * parts[2:]) * scale
    return grad_vel, grad_buoy, now[None], prev[None]


def solution(mesh):
    return jax.shard_map(
        shards,
        mesh=mesh,
        in_specs=(
            P("shot", "gx", "gy"),
            P("shot", "gx", "gy"),
            P("shot", None, None, "gx", "gy"),
            P("shot", None, "gx", "gy"),
            P("shot", None, "gx", "gy"),
            P("shot", None),
            P("shot", None, None),
        ),
        out_specs=(
            P("shot", "gx", "gy"),
            P("shot", "gx", "gy"),
            P("shot", None, "gx", "gy"),
            P("shot", None, "gx", "gy"),
        ),
        check_vma=False,
    )
```
